512 devices in a mesh: row: 32 (over y, x), col: 16 (over z, core).
Axes of the slice: x: 4, y: 8, z: 8, core: 2. Of those that a mesh axis runs over, the one named last changes fastest.
Arguments:
- activations: bfloat16 [576, 8192], P('row', 'col'), may hold values from -6 to 6
- gate_matrix: bfloat16 [8192, 28672], P('col', 'row'), may hold values from -0.0625 to 0.0625
- up_matrix: bfloat16 [8192, 28672], P('col', 'row'), may hold values from -0.0625 to 0.0625
- down_matrix: bfloat16 [28672, 8192], P('row', 'col'), may hold values from -0.03125 to 0.03125
Outputs:
- layer_out: bfloat16 [576, 8192], P('row', 'col')
The draws below stay inside these ranges and needn't reach their ends.
All inputs are finite; a program needn't handle non-finite values.
Results may differ from the reference program's by a relative error of at most 0.0049.
Values may be sent and summed in bfloat16 or wider, within the bound.
No kernel may reach another device: no remote copies, remote signals or barrier semaphores. Data moves between devices by JAX's collectives and lax.ppermute only.
A program may use at most 64 MiB of HBM per device.

```python
import jax
import jax.numpy as jnp

D = 8192
FF = 28672
TOKENS = 576


def levels(rng, extent, shards, least, high):
    def one(dim, parts):
        heights = jax.random.uniform(jax.random.fold_in(jax.random.fold_in(rng, 6), dim), (parts,), jnp.float32, least / len(shards), high / len(shards))
        return jnp.repeat(jnp.exp(heights), extent[dim] // parts).reshape((-1,) + (1,) * (len(extent) - dim - 1))

    level = one(*shards[0])
    for cut in shards[1:]:
        level = level * one(*cut)
    return level


def gaussian(rng, shape, width, bound, shards=(), kind=jnp.bfloat16):
    drawn = width * jax.random.normal(rng, shape, jnp.float32)
    if shards:
        drawn = drawn * levels(rng, shape, shards, -0.22, 0.18)
    return jnp.clip(drawn, -bound, bound).astype(kind)


def setup_inputs(seed: int = 0) -> dict:
    seeds = jax.random.split(jax.random.key(seed), 5)
    return {
        "activations": gaussian(seeds[0], (TOKENS, D), 1.0, 6.0, ((0, 32), (1, 16))),
        "gate_matrix": gaussian(seeds[1], (D, FF), D ** -0.5, 0.0625, ((0, 16), (1, 32))),
        "up_matrix": gaussian(seeds[2], (D, FF), D ** -0.5, 0.0625, ((0, 16), (1, 32))),
        "down_matrix": gaussian(seeds[3], (FF, D), FF ** -0.5, 0.03125, ((0, 32), (1, 16))),
    }


def reference(activations, gate_matrix, up_matrix, down_matrix):
    gate = jnp.dot(activations, gate_matrix, preferred_element_type=jnp.float32)
    up = jnp.dot(activations, up_matrix, preferred_element_type=jnp.float32)
    hidden = (jax.nn.silu(gate) * up).astype(jnp.bfloat16)
    return jnp.dot(hidden, down_matrix, preferred_element_type=jnp.float32).astype(jnp.bfloat16)
```

```python
import functools

import jax
import jax.numpy as jnp
from jax import lax
from jax.experimental import pallas as pl
from jax.experimental.pallas import tpu as pltpu
from jax.sharding import PartitionSpec as P

LANES = 128
VMEM = pltpu.CompilerParams(vmem_limit_bytes=48 * 1024 * 1024)
SCALE = 16.0
DOWN, UP, KEPT = (-1, 4, 2), (1, -2), (0, -3, 3)
NEAR, BELOW, ABOVE = (0, 3, -3), (-1, 2, 4), (1, -2)


def along(axis_size, step):
    return [(i, (i + step) % axis_size) for i in range(axis_size)]


def swap(axis_size):
    return [(i, i ^ 1) for i in range(axis_size)]


def one_hot(rows, columns, tokens, column_tiles, flip):
    r = lax.broadcasted_iota(jnp.int32, (rows, columns), 0)
    c = lax.broadcasted_iota(jnp.int32, (rows, columns), 1)
    if flip:
        r, c = c, r
    return (c == (r % tokens) * column_tiles + r // tokens).astype(jnp.bfloat16)


def unpack_kernel(order, z_ref, own_ref, other_ref, out_ref):
    blocks = len(order)
    sources, rows = own_ref.shape[0] // blocks, own_ref.shape[1]
    tokens = out_ref.shape[1]
    tiles = sources * rows // tokens
    place = one_hot(tiles * tokens, sources * rows, tokens, tiles, False)
    width = tiles * LANES
    for j, offset in enumerate(order):
        block = lax.rem(z_ref[0] + offset + blocks, blocks)
        start = block * sources
        own = own_ref[pl.ds(start, sources)].reshape(sources * rows, LANES)
        other = other_ref[pl.ds(start, sources)].reshape(sources * rows, LANES)
        both = jnp.concatenate([own, other], axis=1)
        moved = jnp.dot(place, both, preferred_element_type=jnp.float32).astype(
            jnp.bfloat16
        )
        for q in range(tiles):
            part = moved[q * tokens : (q + 1) * tokens]
            out_ref[j, :, q * LANES : (q + 1) * LANES] = part[:, :LANES]
            out_ref[j, :, width + q * LANES : width + (q + 1) * LANES] = part[:, LANES:]


def unpack(order, z, own, other, tokens):
    width = own.shape[0] * own.shape[1] * LANES // (len(order) * tokens)
    return pl.pallas_call(
        functools.partial(unpack_kernel, order),
        out_shape=jax.ShapeDtypeStruct((len(order), tokens, 2 * width), jnp.bfloat16),
        in_specs=[
            pl.BlockSpec(memory_space=pltpu.SMEM),
            pl.BlockSpec(memory_space=pltpu.VMEM),
            pl.BlockSpec(memory_space=pltpu.VMEM),
        ],
        out_specs=pl.BlockSpec(memory_space=pltpu.VMEM),
        compiler_params=VMEM,
    )(z, own, other)


def activate_kernel(core_ref, total_ref, out_ref):
    tokens, width = total_ref.shape
    tiles = width // LANES // 2
    gate = total_ref[:, : tiles * LANES]
    mixed = total_ref[:, tiles * LANES : (tiles + 1) * LANES]
    up = total_ref[:, (tiles + 1) * LANES :]
    whole = (gate / (1 + jnp.exp(-gate)) * up).astype(jnp.bfloat16)
    for q in range(tiles):
        out_ref[:, q * LANES : (q + 1) * LANES] = whole[:, q * LANES : (q + 1) * LANES]
    half = mixed / (1 + jnp.exp(-mixed)) * pltpu.roll(mixed, LANES // 2, 1)
    lane = lax.broadcasted_iota(jnp.int32, (tokens, LANES), 1)
    mine = (lane // (LANES // 2)) == core_ref[0]
    out_ref[:, tiles * LANES :] = jnp.where(mine, half, 0.0).astype(jnp.bfloat16)


def activate(core, total):
    tokens, width = total.shape
    return pl.pallas_call(
        activate_kernel,
        out_shape=jax.ShapeDtypeStruct(
            (tokens, (width // LANES // 2 + 1) * LANES), jnp.bfloat16
        ),
        in_specs=[
            pl.BlockSpec(memory_space=pltpu.SMEM),
            pl.BlockSpec(memory_space=pltpu.VMEM),
        ],
        out_specs=pl.BlockSpec(memory_space=pltpu.VMEM),
        compiler_params=VMEM,
    )(core, total)


def down_kernel(groups, where_ref, *refs):
    n = len(groups)
    mine, theirs = refs[:n], refs[n : 2 * n]
    weight_ref, out_ref, hidden_ref = refs[2 * n :]
    blocks = sum(len(g) for g in groups)
    tokens = mine[0].shape[1]
    tiles = mine[0].shape[2] // LANES - 1
    sources, rows = out_ref.shape[0] // blocks, out_ref.shape[1]
    first = where_ref[1] == 0
    at = 0
    for a_ref, b_ref, group in zip(mine, theirs, groups):
        for j in range(len(group)):
            a, b = a_ref[j], b_ref[j]
            low, high = jnp.where(first, a, b), jnp.where(first, b, a)
            split = tiles * LANES
            hidden_ref[at, :, :split] = low[:, :split]
            hidden_ref[at, :, split : split + LANES] = low[:, split:] + high[:, split:]
            hidden_ref[at, :, split + LANES :] = high[:, :split]
            at += 1
    column_tiles = weight_ref.shape[1] // LANES
    place = one_hot(sources * rows, column_tiles * tokens, tokens, column_tiles, True)
    weight = weight_ref[...]
    at = 0
    for group in groups:
        for offset in group:
            result = jnp.dot(
                hidden_ref[at], weight, preferred_element_type=jnp.float32
            ).astype(jnp.bfloat16)
            stacked = jnp.concatenate(
                [result[:, q * LANES : (q + 1) * LANES] for q in range(column_tiles)],
                axis=0,
            )
            packed = jnp.dot(
                place, stacked, preferred_element_type=jnp.float32
            ).astype(jnp.bfloat16)
            block = lax.rem(where_ref[0] + offset + blocks, blocks)
            out_ref[pl.ds(block * sources, sources)] = packed.reshape(
                sources, rows, LANES
            )
            at += 1


def down(groups, where, mine, theirs, weight, sources, rows):
    blocks = sum(len(g) for g in groups)
    tokens = mine[0].shape[1]
    whole = pl.BlockSpec(memory_space=pltpu.VMEM)
    return pl.pallas_call(
        functools.partial(down_kernel, groups),
        out_shape=jax.ShapeDtypeStruct((sources * blocks, rows, LANES), jnp.bfloat16),
        in_specs=[pl.BlockSpec(memory_space=pltpu.SMEM)]
        + [whole] * (2 * len(groups) + 1),
        out_specs=whole,
        scratch_shapes=[pltpu.VMEM((blocks, tokens, weight.shape[0]), jnp.bfloat16)],
        compiler_params=VMEM,
    )(where, *mine, *theirs, weight)


def sum_kernel(shares_ref, out_ref):
    total = shares_ref[0].astype(jnp.float32)
    for r in range(1, shares_ref.shape[0]):
        total += shares_ref[r].astype(jnp.float32)
    out_ref[...] = total.astype(jnp.bfloat16)


def add_up(shares):
    return pl.pallas_call(
        sum_kernel,
        out_shape=jax.ShapeDtypeStruct(shares.shape[1:], jnp.bfloat16),
        in_specs=[pl.BlockSpec(memory_space=pltpu.VMEM)],
        out_specs=pl.BlockSpec(memory_space=pltpu.VMEM),
        compiler_params=VMEM,
    )(shares)


def split_columns(gate, up):
    width = gate.shape[1]
    half, tile = width // 2, width // 2 // LANES * LANES
    low = [gate[:, :half], up[:, tile:half], up[:, :tile]]
    high = [
        gate[:, width - tile :],
        up[:, half : width - tile],
        gate[:, half : width - tile],
        up[:, width - tile :],
    ]
    return jnp.concatenate(low, axis=1), jnp.concatenate(high, axis=1)


def shards(activations, gate_matrix, up_matrix, down_matrix):
    n_row, n_col = lax.axis_size("row"), lax.axis_size("col")
    depth = n_col // 2
    me = lax.axis_index("col")
    z, core = me // 2, me % 2
    own_tokens, width = activations.shape
    tokens = n_row * own_tokens // depth
    rows = own_tokens * width // LANES
    shift = lambda x, step: lax.ppermute(x, "col", along(n_col, 2 * step))
    other_core = lambda x: lax.ppermute(x, "col", swap(n_col))

    packed = activations.reshape(rows, LANES)
    spread = jnp.broadcast_to(packed[None], (n_row, rows, LANES))
    got = lax.all_to_all(spread, "row", 0, 0, tiled=True)

    low, high = split_columns(gate_matrix, up_matrix)
    kept = jnp.where(core == 0, low, high)
    weights = jnp.concatenate(
        [kept, other_core(jnp.where(core == 0, high, low))], axis=0
    )

    order = DOWN + UP + KEPT
    inputs = unpack(order, z.reshape(1), got, other_core(got), tokens)

    def partial(first, count):
        term = jnp.dot(
            inputs[first : first + count].reshape(count * tokens, 2 * width),
            weights,
            preferred_element_type=jnp.float32,
        )
        return (term * SCALE).reshape(count, tokens, weights.shape[1])

    narrow = lambda x: x.astype(jnp.float16)
    wide = lambda x: x.astype(jnp.float32)
    from_above = wide(shift(narrow(partial(0, 3)), -1))
    from_below = wide(shift(narrow(partial(3, 2)), 1))
    stay = partial(5, 3)
    to_below = shift(narrow(stay[1] + from_above[1] + from_below[1]), -3)
    to_above = shift(narrow(stay[2] + from_above[2]), 3)
    total = stay[0] + from_above[0] + from_below[0] + (wide(to_below) + wide(to_above))

    hidden = activate(core.reshape(1), total * (1 / SCALE))
    near = jnp.stack([hidden, shift(hidden, -3), shift(hidden, 3)])
    below = shift(near, 1)
    above = shift(jnp.stack([near[0], near[2]]), -1)
    mine = (near, below, above)
    theirs = tuple(other_core(x) for x in mine)
    share = down(
        (NEAR, BELOW, ABOVE),
        jnp.stack([z, core]),
        mine,
        theirs,
        down_matrix,
        n_row // depth,
        rows,
    )
    shares = lax.all_to_all(share, "row", 0, 0, tiled=True)
    return add_up(shares).reshape(own_tokens, width)


def solution(mesh):
    placed = (P("row", "col"), P("col", "row"), P("col", "row"), P("row", "col"))
    return jax.shard_map(
        shards, mesh=mesh, in_specs=placed, out_specs=P("row", "col"), check_vma=False
    )
```

```python
import functools

import jax
import jax.numpy as jnp
from jax import lax
from jax.experimental import pallas as pl
from jax.experimental.pallas import tpu as pltpu
from jax.sharding import PartitionSpec as P

LANES = 128
MAIN = 16
EXTRA = 2
PAIR = 2
STRIDE = 48
LIMIT = pltpu.CompilerParams(vmem_limit_bytes=48 * 1024 * 1024)
SCALAR = pl.BlockSpec(memory_space=pltpu.SMEM)
WHOLE = pl.BlockSpec(memory_space=pltpu.VMEM)
SCALE = 16.0


def lanes(q):
    return slice(q * LANES, (q + 1) * LANES)


def rows_of(q, count):
    return slice(q * count, (q + 1) * count)


def gather_extra(tiles, shift_of):
    row = lax.broadcasted_iota(jnp.int32, tiles[0].shape, 0) // EXTRA
    out = tiles[0] if shift_of(0) % 8 == 0 else pltpu.roll(tiles[0], shift_of(0) % 8, 0)
    for q in range(1, len(tiles)):
        moved = tiles[q]
        if shift_of(q) % 8:
            moved = pltpu.roll(moved, shift_of(q) % 8, 0)
        out = jnp.where(row == q, moved, out)
    return out


def spread_kernel(x_ref, out_ref):
    x = x_ref[...].astype(jnp.float32)
    tiles = x.shape[1] // LANES
    for q in range(tiles):
        for r in range(out_ref.shape[0]):
            out_ref[r, rows_of(q, MAIN), :] = x_ref[:MAIN, lanes(q)]
    tail = jnp.concatenate(
        [x[MAIN:, lanes(q)] for q in range(tiles)], axis=0
    ).astype(jnp.bfloat16)
    for r in range(out_ref.shape[0]):
        out_ref[r, tiles * MAIN :, :] = tail


def spread(x, copies):
    rows = x.shape[0] * x.shape[1] // LANES
    return pl.pallas_call(
        spread_kernel,
        out_shape=jax.ShapeDtypeStruct((copies, rows, LANES), x.dtype),
        in_specs=[WHOLE],
        out_specs=WHOLE,
        compiler_params=LIMIT,
    )(x)


def up_kernel(core_ref, own_ref, other_ref, *refs):
    gate_own, gate_other, up_own, up_other, out_ref, held = refs
    blocks = out_ref.shape[0]
    tiles = own_ref.shape[1] // (MAIN + EXTRA)
    width = tiles * LANES
    wide_tiles = gate_own.shape[1] // LANES
    span = PAIR * MAIN
    r = lax.broadcasted_iota(jnp.int32, (tiles * 8, PAIR * 8), 0)
    c = lax.broadcasted_iota(jnp.int32, (tiles * 8, PAIR * 8), 1)
    n = (r % 8) % (PAIR * EXTRA)
    place = c == (n // EXTRA) * 8 + (r // 8) * EXTRA + n % EXTRA
    place = place.astype(jnp.bfloat16)
    for b in range(blocks):
        tails = []
        for s in range(PAIR):
            own = own_ref[b * 2 * PAIR + core_ref[0] * PAIR + s]
            other = other_ref[b, s]
            for q in range(tiles):
                held[b, rows_of(s, MAIN), lanes(q)] = own[rows_of(q, MAIN)]
                held[b, rows_of(s, MAIN), lanes(tiles + q)] = other[rows_of(q, MAIN)]
            tails.append(
                jnp.concatenate([own[tiles * MAIN :], other[tiles * MAIN :]], axis=1)
            )
        moved = jnp.dot(
            place,
            jnp.concatenate(tails, axis=0),
            preferred_element_type=jnp.float32,
        ).astype(jnp.bfloat16)
        for q in range(tiles):
            held[b, span : span + 8, lanes(q)] = moved[rows_of(q, 8), :LANES]
            held[b, span : span + 8, lanes(tiles + q)] = moved[rows_of(q, 8), LANES:]
    left = held[:, :, :width].reshape(blocks * STRIDE, width)
    right = held[:, :, width:].reshape(blocks * STRIDE, width)
    top = lax.broadcasted_iota(jnp.int32, (8, LANES), 0) < PAIR * EXTRA

    def dot(x, w):
        return jnp.dot(x, w, preferred_element_type=jnp.float32)

    gate = (dot(left, gate_own[...]) + dot(right, gate_other[...])) * SCALE
    up = (dot(left, up_own[...]) + dot(right, up_other[...])) * SCALE
    for b in range(blocks):
        at = b * STRIDE
        for j in range(wide_tiles):
            out_ref[b, rows_of(j, span), :] = gate[at : at + span, lanes(j)]
            out_ref[b, rows_of(wide_tiles + j, span), :] = up[at : at + span, lanes(j)]
            mixed = jnp.where(
                top,
                gate[at + span : at + span + 8, lanes(j)],
                up[at + span : at + span + 8, lanes(j)],
            )
            start = 2 * wide_tiles * span + 8 * j
            out_ref[b, start : start + 8, :] = mixed


def up_product(core, own, other, gate_own, gate_other, up_own, up_other):
    blocks = other.shape[0]
    tiles = own.shape[1] // (MAIN + EXTRA)
    rows = PAIR * (MAIN + EXTRA) * 2 * gate_own.shape[1] // LANES
    return pl.pallas_call(
        up_kernel,
        out_shape=jax.ShapeDtypeStruct((blocks, rows, LANES), jnp.float32),
        in_specs=[SCALAR] + [WHOLE] * 6,
        out_specs=WHOLE,
        scratch_shapes=[pltpu.VMEM((blocks, STRIDE, 2 * tiles * LANES), jnp.bfloat16)],
        compiler_params=LIMIT,
    )(core, own, other, gate_own, gate_other, up_own, up_other)


def activate_kernel(sum_ref, out_ref):
    span = PAIR * MAIN
    wide_tiles = out_ref.shape[1] // LANES
    for j in range(wide_tiles):
        gate = sum_ref[rows_of(j, span), :]
        up = sum_ref[rows_of(wide_tiles + j, span), :]
        out_ref[:span, lanes(j)] = (gate / (1 + jnp.exp(-gate)) * up).astype(
            jnp.bfloat16
        )
        start = 2 * wide_tiles * span + 8 * j
        mixed = sum_ref[start : start + 8, :]
        tail = mixed / (1 + jnp.exp(-mixed)) * pltpu.roll(mixed, PAIR * EXTRA, 0)
        out_ref[span:, lanes(j)] = tail[: PAIR * EXTRA].astype(jnp.bfloat16)


def activate(total, hidden_width):
    return pl.pallas_call(
        activate_kernel,
        out_shape=jax.ShapeDtypeStruct(
            (PAIR * (MAIN + EXTRA), hidden_width), jnp.bfloat16
        ),
        in_specs=[WHOLE],
        out_specs=WHOLE,
        compiler_params=LIMIT,
    )(total)


def down_kernel(hidden_ref, weight_ref, out_ref, held):
    blocks, count = hidden_ref.shape[:2]
    span = PAIR * MAIN
    for b in range(blocks):
        held[b, :count, :] = hidden_ref[b]
    tiles = weight_ref.shape[1] // LANES
    result = jnp.dot(
        held[...].reshape(blocks * STRIDE, held.shape[2]),
        weight_ref[...],
        preferred_element_type=jnp.float32,
    )
    for b in range(blocks):
        at = b * STRIDE
        ends = [result[at + span : at + span + 8, lanes(q)] for q in range(tiles)]
        for s in range(PAIR):
            for q in range(tiles):
                out_ref[b * PAIR + s, rows_of(q, MAIN), :] = result[
                    at + s * MAIN : at + (s + 1) * MAIN, lanes(q)
                ].astype(jnp.bfloat16)
            tail = gather_extra(ends, lambda q: (q - s) * EXTRA)
            out_ref[b * PAIR + s, tiles * MAIN :, :] = tail.astype(jnp.bfloat16)


def down_product(hidden, weight):
    blocks, count, width = hidden.shape
    rows = (MAIN + EXTRA) * weight.shape[1] // LANES
    return pl.pallas_call(
        down_kernel,
        out_shape=jax.ShapeDtypeStruct((PAIR * blocks, rows, LANES), jnp.bfloat16),
        in_specs=[WHOLE] * 2,
        out_specs=WHOLE,
        scratch_shapes=[pltpu.VMEM((blocks, STRIDE, width), jnp.bfloat16)],
        compiler_params=LIMIT,
    )(hidden, weight)


def finish_kernel(shares_ref, out_ref):
    tiles = out_ref.shape[1] // LANES
    total = shares_ref[0].astype(jnp.float32)
    for r in range(1, shares_ref.shape[0]):
        total += shares_ref[r].astype(jnp.float32)
    for q in range(tiles):
        out_ref[:MAIN, lanes(q)] = total[rows_of(q, MAIN)].astype(jnp.bfloat16)
        tail = total[tiles * MAIN + q * EXTRA : tiles * MAIN + (q + 1) * EXTRA]
        out_ref[MAIN:, lanes(q)] = tail.astype(jnp.bfloat16)


def finish(shares):
    width = shares.shape[1] // (MAIN + EXTRA) * LANES
    return pl.pallas_call(
        finish_kernel,
        out_shape=jax.ShapeDtypeStruct((MAIN + EXTRA, width), jnp.bfloat16),
        in_specs=[WHOLE],
        out_specs=WHOLE,
        compiler_params=LIMIT,
    )(shares)


def shards(activations, gate_matrix, up_matrix, down_matrix):
    n_row, n_col = lax.axis_size("row"), lax.axis_size("col")
    depth = n_col // 2
    core = lax.axis_index("col") % 2
    same_core = [[2 * i + k for i in range(depth)] for k in range(2)]

    def other_core(x):
        return lax.ppermute(x, "col", [(i, i ^ 1) for i in range(n_col)])

    own = lax.all_to_all(spread(activations, n_row), "row", 0, 0, tiled=True)
    gate_other, up_other = other_core(gate_matrix), other_core(up_matrix)
    by_core = own.reshape(depth, 2, PAIR, *own.shape[1:])
    give = lax.dynamic_index_in_dim(by_core, 1 - core, 1, keepdims=False)
    terms = up_product(
        core.reshape(1),
        own,
        other_core(give),
        gate_matrix,
        gate_other,
        up_matrix,
        up_other,
    )
    terms = lax.all_to_all(
        terms.astype(jnp.float16),
        "col",
        0,
        0,
        axis_index_groups=same_core,
        tiled=True,
    )
    total = jnp.sum(terms.astype(jnp.float32), axis=0) * (1 / SCALE)
    hidden = activate(total, gate_matrix.shape[1])
    gathered = lax.all_gather(hidden, "col", axis=0, tiled=False)
    share = down_product(gathered, down_matrix)
    return finish(lax.all_to_all(share, "row", 0, 0, tiled=True))


def solution(mesh):
    placed = (P("row", "col"), P("col", "row"), P("col", "row"), P("row", "col"))
    return jax.shard_map(
        shards, mesh=mesh, in_specs=placed, out_specs=P("row", "col"), check_vma=False
    )
```

```python
import functools

import jax
import jax.numpy as jnp
from jax import lax
from jax.experimental import pallas as pl
from jax.experimental.pallas import tpu as pltpu
from jax.sharding import PartitionSpec as P

LANES = 128
MAIN = 16
EXTRA = 2
PAIR = 2
STRIDE = 48
LIMIT = pltpu.CompilerParams(vmem_limit_bytes=24 * 1024 * 1024)
SCALAR = pl.BlockSpec(memory_space=pltpu.SMEM)
WHOLE = pl.BlockSpec(memory_space=pltpu.VMEM)
SCALE = 16.0


def lanes(q):
    return slice(q * LANES, (q + 1) * LANES)


def rows_of(q, count):
    return slice(q * count, (q + 1) * count)


def gather_extra(tiles, shift_of):
    row = lax.broadcasted_iota(jnp.int32, tiles[0].shape, 0) // EXTRA
    out = tiles[0] if shift_of(0) % 8 == 0 else pltpu.roll(tiles[0], shift_of(0) % 8, 0)
    for q in range(1, len(tiles)):
        moved = tiles[q]
        if shift_of(q) % 8:
            moved = pltpu.roll(moved, shift_of(q) % 8, 0)
        out = jnp.where(row == q, moved, out)
    return out


def spread_kernel(x_ref, out_ref):
    x = x_ref[...].astype(jnp.float32)
    tiles = x.shape[1] // LANES
    for q in range(tiles):
        for r in range(out_ref.shape[0]):
            out_ref[r, rows_of(q, MAIN), :] = x_ref[:MAIN, lanes(q)]
    tail = jnp.concatenate(
        [x[MAIN:, lanes(q)] for q in range(tiles)], axis=0
    ).astype(jnp.bfloat16)
    for r in range(out_ref.shape[0]):
        out_ref[r, tiles * MAIN :, :] = tail


def spread(x, copies):
    rows = x.shape[0] * x.shape[1] // LANES
    return pl.pallas_call(
        spread_kernel,
        out_shape=jax.ShapeDtypeStruct((copies, rows, LANES), x.dtype),
        in_specs=[WHOLE],
        out_specs=WHOLE,
        compiler_params=LIMIT,
    )(x)


def add_product(own_at, gate_ref, up_ref, base_ref, out_ref, held):
    blocks = out_ref.shape[0]
    tiles = held.shape[1] // LANES
    wide_tiles = gate_ref.shape[1] // LANES
    span = PAIR * MAIN
    shape = (tiles * blocks * 8, blocks * PAIR * 8)
    r = lax.broadcasted_iota(jnp.int32, shape, 0)
    c = lax.broadcasted_iota(jnp.int32, shape, 1)
    q, b, n = r // (blocks * 8), r // 8 % blocks, r % (PAIR * EXTRA)
    place = c == b * PAIR * 8 + n // EXTRA * 8 + q * EXTRA + n % EXTRA
    tails = []
    for b in range(blocks):
        for s in range(PAIR):
            block = own_at(b, s)
            for q in range(tiles):
                at = b * span + s * MAIN
                held[at : at + MAIN, lanes(q)] = block[rows_of(q, MAIN)]
            tails.append(block[tiles * MAIN :])
    moved = jnp.dot(
        place.astype(jnp.bfloat16),
        jnp.concatenate(tails, axis=0),
        preferred_element_type=jnp.float32,
    ).astype(jnp.bfloat16)
    for q in range(tiles):
        held[blocks * span :, lanes(q)] = moved[rows_of(q, blocks * 8)]
    top = lax.broadcasted_iota(jnp.int32, (8, LANES), 0) < PAIR * EXTRA
    x = held[...]
    for first in range(0, wide_tiles, 2):
        count = min(2, wide_tiles - first)
        columns = slice(first * LANES, (first + count) * LANES)
        gate = jnp.dot(x, gate_ref[:, columns], preferred_element_type=jnp.float32)
        up = jnp.dot(x, up_ref[:, columns], preferred_element_type=jnp.float32)
        for i in range(count):
            j = first + i
            for b in range(blocks):
                at = slice(b * span, (b + 1) * span)
                end = slice(blocks * span + b * 8, blocks * span + b * 8 + 8)
                start = 2 * wide_tiles * span + 8 * j
                mixed = jnp.where(top, gate[end, lanes(i)], up[end, lanes(i)])
                for where, value in (
                    (rows_of(j, span), gate[at, lanes(i)]),
                    (rows_of(wide_tiles + j, span), up[at, lanes(i)]),
                    (slice(start, start + 8), mixed),
                ):
                    if base_ref is not None:
                        value += base_ref[b, where, :]
                    out_ref[b, where, :] = value


def own_kernel(core_ref, own_ref, gate_ref, up_ref, out_ref, held):
    def own_at(b, s):
        return own_ref[b * 2 * PAIR + core_ref[0] * PAIR + s]

    add_product(own_at, gate_ref, up_ref, None, out_ref, held)


def other_kernel(other_ref, gate_ref, up_ref, base_ref, out_ref, held):
    add_product(
        lambda b, s: other_ref[b, s], gate_ref, up_ref, base_ref, out_ref, held
    )


def up_product(kernel, specs, blocks, operands, gate, up, *base):
    rows = PAIR * (MAIN + EXTRA) * 2 * gate.shape[1] // LANES
    held = pltpu.VMEM((blocks * (PAIR * MAIN + 8), gate.shape[0]), jnp.bfloat16)
    return pl.pallas_call(
        kernel,
        out_shape=pltpu.VMEM((blocks, rows, LANES), jnp.float32),
        in_specs=specs + [WHOLE] * (2 + len(base)),
        out_specs=WHOLE,
        scratch_shapes=[held],
        compiler_params=LIMIT,
    )(*operands, gate, up, *base)


def activate_kernel(theirs_ref, mine_ref, out_ref):
    def total(rows):
        return theirs_ref[rows, :] * (1 / SCALE) + mine_ref[rows, :]

    span = PAIR * MAIN
    wide_tiles = out_ref.shape[1] // LANES
    for j in range(wide_tiles):
        gate = total(rows_of(j, span))
        up = total(rows_of(wide_tiles + j, span))
        out_ref[:span, lanes(j)] = (gate / (1 + jnp.exp(-gate)) * up).astype(
            jnp.bfloat16
        )
        start = 2 * wide_tiles * span + 8 * j
        mixed = total(slice(start, start + 8))
        tail = mixed / (1 + jnp.exp(-mixed)) * pltpu.roll(mixed, PAIR * EXTRA, 0)
        out_ref[span:, lanes(j)] = tail[: PAIR * EXTRA].astype(jnp.bfloat16)


def activate(theirs, mine, hidden_width):
    return pl.pallas_call(
        activate_kernel,
        out_shape=jax.ShapeDtypeStruct(
            (PAIR * (MAIN + EXTRA), hidden_width), jnp.bfloat16
        ),
        in_specs=[WHOLE] * 2,
        out_specs=WHOLE,
        compiler_params=LIMIT,
    )(theirs, mine)


def down_kernel(hidden_ref, weight_ref, out_ref, held):
    blocks, count = hidden_ref.shape[:2]
    span = PAIR * MAIN
    for b in range(blocks):
        held[b, :count, :] = hidden_ref[b]
    tiles = weight_ref.shape[1] // LANES
    result = jnp.dot(
        held[...].reshape(blocks * STRIDE, held.shape[2]),
        weight_ref[...],
        preferred_element_type=jnp.float32,
    )
    for b in range(blocks):
        at = b * STRIDE
        ends = [result[at + span : at + span + 8, lanes(q)] for q in range(tiles)]
        for s in range(PAIR):
            for q in range(tiles):
                out_ref[b * PAIR + s, rows_of(q, MAIN), :] = result[
                    at + s * MAIN : at + (s + 1) * MAIN, lanes(q)
                ].astype(jnp.bfloat16)
            tail = gather_extra(ends, lambda q: (q - s) * EXTRA)
            out_ref[b * PAIR + s, tiles * MAIN :, :] = tail.astype(jnp.bfloat16)


def down_product(hidden, weight):
    blocks, count, width = hidden.shape
    rows = (MAIN + EXTRA) * weight.shape[1] // LANES
    return pl.pallas_call(
        down_kernel,
        out_shape=jax.ShapeDtypeStruct((PAIR * blocks, rows, LANES), jnp.bfloat16),
        in_specs=[WHOLE] * 2,
        out_specs=WHOLE,
        scratch_shapes=[pltpu.VMEM((blocks, STRIDE, width), jnp.bfloat16)],
        compiler_params=LIMIT,
    )(hidden, weight)


def finish_kernel(me_ref, mine_ref, shares_ref, out_ref):
    tiles = out_ref.shape[1] // LANES
    total = mine_ref[...]
    for r in range(shares_ref.shape[0]):
        share = shares_ref[r].astype(jnp.float32)
        total += jnp.where(r == me_ref[0], 0.0, share)
    for q in range(tiles):
        out_ref[:MAIN, lanes(q)] = total[rows_of(q, MAIN)].astype(jnp.bfloat16)
        tail = total[tiles * MAIN + q * EXTRA : tiles * MAIN + (q + 1) * EXTRA]
        out_ref[MAIN:, lanes(q)] = tail.astype(jnp.bfloat16)


def finish(me, mine, shares):
    width = shares.shape[1] // (MAIN + EXTRA) * LANES
    return pl.pallas_call(
        finish_kernel,
        out_shape=jax.ShapeDtypeStruct((MAIN + EXTRA, width), jnp.bfloat16),
        in_specs=[SCALAR, WHOLE, WHOLE],
        out_specs=WHOLE,
        compiler_params=LIMIT,
    )(me, mine, shares)


def shards(activations, gate_matrix, up_matrix, down_matrix):
    n_row, n_col = lax.axis_size("row"), lax.axis_size("col")
    depth = n_col // 2
    core = lax.axis_index("col") % 2
    same_core = [[2 * i + k for i in range(depth)] for k in range(2)]

    def other_core(x):
        return lax.ppermute(x, "col", [(i, i ^ 1) for i in range(n_col)])

    own = lax.all_to_all(spread(activations, n_row), "row", 0, 0, tiled=True)
    gate_other, up_other = other_core(gate_matrix), other_core(up_matrix)
    by_core = own.reshape(depth, 2, PAIR, *own.shape[1:])
    give = lax.dynamic_index_in_dim(by_core, 1 - core, 1, keepdims=False)
    other = other_core(give)
    terms = up_product(
        own_kernel,
        [SCALAR, WHOLE],
        depth,
        (core.reshape(1), own),
        gate_matrix,
        up_matrix,
    )
    terms = up_product(
        other_kernel, [WHOLE], depth, (other,), gate_other, up_other, terms
    )
    place = lax.axis_index("col") // 2
    mine = lax.dynamic_index_in_dim(terms, place, 0, keepdims=False)
    arrived = lax.all_to_all(
        (terms * SCALE).astype(jnp.float16),
        "col",
        0,
        0,
        axis_index_groups=same_core,
        tiled=True,
    ).astype(jnp.float32)
    here = jnp.arange(depth)[:, None, None] == place
    theirs = jnp.sum(jnp.where(here, 0, arrived), axis=0)
    hidden = activate(theirs, mine, gate_matrix.shape[1])
    gathered = lax.all_gather(hidden, "col", axis=0, tiled=False)
    share = down_product(gathered, down_matrix)
    r = lax.axis_index("row")
    mine = lax.dynamic_index_in_dim(share, r, 0, keepdims=False).astype(jnp.float32)
    return finish(r.reshape(1), mine, lax.all_to_all(share, "row", 0, 0, tiled=True))


def solution(mesh):
    placed = (P("row", "col"), P("col", "row"), P("col", "row"), P("row", "col"))
    return jax.shard_map(
        shards, mesh=mesh, in_specs=placed, out_specs=P("row", "col"), check_vma=False
    )
```

```python
import functools

import jax
import jax.numpy as jnp
from jax import lax
from jax.experimental import pallas as pl
from jax.experimental.pallas import tpu as pltpu
from jax.sharding import PartitionSpec as P

LANES = 128
MAIN = 16
EXTRA = 2
PAIR = 2
STRIDE = 48
LIMIT = pltpu.CompilerParams(vmem_limit_bytes=8 * 1024 * 1024)
SCALAR = pl.BlockSpec(memory_space=pltpu.SMEM)
WHOLE = pl.BlockSpec(memory_space=pltpu.VMEM)
SCALE = 16.0
ROW, COL = ("y", "x"), ("z", "core")
ALONG_X = 4


def lanes(q):
    return slice(q * LANES, (q + 1) * LANES)


def rows_of(q, count):
    return slice(q * count, (q + 1) * count)


def gather_extra(tiles, shift_of):
    row = lax.broadcasted_iota(jnp.int32, tiles[0].shape, 0) // EXTRA
    out = tiles[0] if shift_of(0) % 8 == 0 else pltpu.roll(tiles[0], shift_of(0) % 8, 0)
    for q in range(1, len(tiles)):
        moved = tiles[q]
        if shift_of(q) % 8:
            moved = pltpu.roll(moved, shift_of(q) % 8, 0)
        out = jnp.where(row == q, moved, out)
    return out


def spread_kernel(x_ref, out_ref):
    x = x_ref[...].astype(jnp.float32)
    tiles = x.shape[1] // LANES
    for q in range(tiles):
        for r in range(out_ref.shape[0]):
            out_ref[r, rows_of(q, MAIN), :] = x_ref[:MAIN, lanes(q)]
    tail = jnp.concatenate(
        [x[MAIN:, lanes(q)] for q in range(tiles)], axis=0
    ).astype(jnp.bfloat16)
    for r in range(out_ref.shape[0]):
        out_ref[r, tiles * MAIN :, :] = tail


def spread(x, copies):
    rows = x.shape[0] * x.shape[1] // LANES
    return pl.pallas_call(
        spread_kernel,
        out_shape=jax.ShapeDtypeStruct((copies, rows, LANES), x.dtype),
        in_specs=[WHOLE],
        out_specs=WHOLE,
        compiler_params=LIMIT,
    )(x)


def add_product(own_at, gate_ref, up_ref, base_ref, out_ref, held):
    blocks = out_ref.shape[0]
    tiles = held.shape[1] // LANES
    wide_tiles = gate_ref.shape[1] // LANES
    span = PAIR * MAIN
    shape = (tiles * blocks * 8, blocks * PAIR * 8)
    r = lax.broadcasted_iota(jnp.int32, shape, 0)
    c = lax.broadcasted_iota(jnp.int32, shape, 1)
    q, b, n = r // (blocks * 8), r // 8 % blocks, r % (PAIR * EXTRA)
    place = c == b * PAIR * 8 + n // EXTRA * 8 + q * EXTRA + n % EXTRA
    tails = []
    for b in range(blocks):
        for s in range(PAIR):
            block = own_at(b, s)
            for q in range(tiles):
                at = b * span + s * MAIN
                held[at : at + MAIN, lanes(q)] = block[rows_of(q, MAIN)]
            tails.append(block[tiles * MAIN :])
    moved = jnp.dot(
        place.astype(jnp.bfloat16),
        jnp.concatenate(tails, axis=0),
        preferred_element_type=jnp.float32,
    ).astype(jnp.bfloat16)
    for q in range(tiles):
        held[blocks * span :, lanes(q)] = moved[rows_of(q, blocks * 8)]
    top = lax.broadcasted_iota(jnp.int32, (8, LANES), 0) < PAIR * EXTRA
    x = held[...]
    for first in range(0, wide_tiles, 2):
        count = min(2, wide_tiles - first)
        columns = slice(first * LANES, (first + count) * LANES)
        gate = jnp.dot(x, gate_ref[:, columns], preferred_element_type=jnp.float32)
        up = jnp.dot(x, up_ref[:, columns], preferred_element_type=jnp.float32)
        for i in range(count):
            j = first + i
            for b in range(blocks):
                at = slice(b * span, (b + 1) * span)
                end = slice(blocks * span + b * 8, blocks * span + b * 8 + 8)
                start = 2 * wide_tiles * span + 8 * j
                mixed = jnp.where(top, gate[end, lanes(i)], up[end, lanes(i)])
                for where, value in (
                    (rows_of(j, span), gate[at, lanes(i)]),
                    (rows_of(wide_tiles + j, span), up[at, lanes(i)]),
                    (slice(start, start + 8), mixed),
                ):
                    if base_ref is not None:
                        value += base_ref[b, where, :]
                    out_ref[b, where, :] = value


def own_kernel(core_ref, own_ref, gate_ref, up_ref, out_ref, held):
    def own_at(b, s):
        return own_ref[b * 2 * PAIR + core_ref[0] * PAIR + s]

    add_product(own_at, gate_ref, up_ref, None, out_ref, held)


def other_kernel(other_ref, gate_ref, up_ref, base_ref, out_ref, held):
    add_product(
        lambda b, s: other_ref[b, s], gate_ref, up_ref, base_ref, out_ref, held
    )


def up_product(kernel, specs, blocks, operands, gate, up, *base):
    rows = PAIR * (MAIN + EXTRA) * 2 * gate.shape[1] // LANES
    held = pltpu.VMEM((blocks * (PAIR * MAIN + 8), gate.shape[0]), jnp.bfloat16)
    return pl.pallas_call(
        kernel,
        out_shape=pltpu.VMEM((blocks, rows, LANES), jnp.float32),
        in_specs=specs + [WHOLE] * (2 + len(base)),
        out_specs=WHOLE,
        scratch_shapes=[held],
        compiler_params=LIMIT,
    )(*operands, gate, up, *base)


def activate_kernel(sum_ref, out_ref):
    def total(rows):
        return sum_ref[rows, :] * (1 / SCALE)

    span = PAIR * MAIN
    wide_tiles = out_ref.shape[1] // LANES
    for j in range(wide_tiles):
        gate = total(rows_of(j, span))
        up = total(rows_of(wide_tiles + j, span))
        out_ref[:span, lanes(j)] = (gate / (1 + jnp.exp(-gate)) * up).astype(
            jnp.bfloat16
        )
        start = 2 * wide_tiles * span + 8 * j
        mixed = total(slice(start, start + 8))
        tail = mixed / (1 + jnp.exp(-mixed)) * pltpu.roll(mixed, PAIR * EXTRA, 0)
        out_ref[span:, lanes(j)] = tail[: PAIR * EXTRA].astype(jnp.bfloat16)


def activate(total, hidden_width):
    return pl.pallas_call(
        activate_kernel,
        out_shape=jax.ShapeDtypeStruct(
            (PAIR * (MAIN + EXTRA), hidden_width), jnp.bfloat16
        ),
        in_specs=[WHOLE],
        out_specs=WHOLE,
        compiler_params=LIMIT,
    )(total)


def down_kernel(hidden_ref, weight_ref, out_ref, held):
    blocks, count = hidden_ref.shape[:2]
    span = PAIR * MAIN
    for b in range(blocks):
        held[b, :count, :] = hidden_ref[b]
    tiles = weight_ref.shape[1] // LANES
    result = jnp.dot(
        held[...].reshape(blocks * STRIDE, held.shape[2]),
        weight_ref[...],
        preferred_element_type=jnp.float32,
    )
    for b in range(blocks):
        at = b * STRIDE
        ends = [result[at + span : at + span + 8, lanes(q)] for q in range(tiles)]
        for s in range(PAIR):
            for q in range(tiles):
                out_ref[b * PAIR + s, rows_of(q, MAIN), :] = result[
                    at + s * MAIN : at + (s + 1) * MAIN, lanes(q)
                ].astype(jnp.bfloat16)
            tail = gather_extra(ends, lambda q: (q - s) * EXTRA)
            out_ref[b * PAIR + s, tiles * MAIN :, :] = tail.astype(jnp.bfloat16)


def down_product(hidden, weight):
    blocks, count, width = hidden.shape
    rows = (MAIN + EXTRA) * weight.shape[1] // LANES
    return pl.pallas_call(
        down_kernel,
        out_shape=jax.ShapeDtypeStruct((PAIR * blocks, rows, LANES), jnp.bfloat16),
        in_specs=[WHOLE] * 2,
        out_specs=WHOLE,
        scratch_shapes=[pltpu.VMEM((blocks, STRIDE, width), jnp.bfloat16)],
        compiler_params=LIMIT,
    )(hidden, weight)


def finish_kernel(shares_ref, out_ref):
    tiles = out_ref.shape[1] // LANES
    total = shares_ref[0].astype(jnp.float32)
    for r in range(1, shares_ref.shape[0]):
        total += shares_ref[r].astype(jnp.float32)
    for q in range(tiles):
        out_ref[:MAIN, lanes(q)] = total[rows_of(q, MAIN)].astype(jnp.bfloat16)
        tail = total[tiles * MAIN + q * EXTRA : tiles * MAIN + (q + 1) * EXTRA]
        out_ref[MAIN:, lanes(q)] = tail.astype(jnp.bfloat16)


def finish(shares):
    width = shares.shape[1] // (MAIN + EXTRA) * LANES
    return pl.pallas_call(
        finish_kernel,
        out_shape=jax.ShapeDtypeStruct((MAIN + EXTRA, width), jnp.bfloat16),
        in_specs=[WHOLE],
        out_specs=WHOLE,
        compiler_params=LIMIT,
    )(shares)


def shards(activations, gate_matrix, up_matrix, down_matrix):
    n_row, depth = lax.axis_size(ROW), lax.axis_size("z")
    core = lax.axis_index("core")

    def other_core(x):
        return lax.ppermute(x, "core", [(0, 1), (1, 0)])

    own = lax.all_to_all(spread(activations, n_row), ROW, 0, 0, tiled=True)
    gate_other, up_other = other_core(gate_matrix), other_core(up_matrix)
    by_core = own.reshape(depth, 2, PAIR, *own.shape[1:])
    give = lax.dynamic_index_in_dim(by_core, 1 - core, 1, keepdims=False)
    other = other_core(give)
    terms = up_product(
        own_kernel,
        [SCALAR, WHOLE],
        depth,
        (core.reshape(1), own),
        gate_matrix,
        up_matrix,
    )
    terms = up_product(
        other_kernel, [WHOLE], depth, (other,), gate_other, up_other, terms
    )
    arrived = lax.all_to_all(
        (terms * SCALE).astype(jnp.float16), "z", 0, 0, tiled=True
    )
    total = jnp.sum(arrived.astype(jnp.float32), axis=0)
    hidden = activate(total, gate_matrix.shape[1])
    gathered = lax.all_gather(hidden, COL, axis=0, tiled=False)
    share = down_product(gathered, down_matrix)
    return finish(lax.all_to_all(share, ROW, 0, 0, tiled=True))


def solution(mesh):
    n_row, n_col = mesh.devices.shape
    devices = mesh.devices.reshape(n_row // ALONG_X, ALONG_X, n_col // 2, 2)
    chips = jax.sharding.Mesh(devices, ROW + COL)
    placed = (P(ROW, COL), P(COL, ROW), P(COL, ROW), P(ROW, COL))
    return jax.shard_map(
        shards, mesh=chips, in_specs=placed, out_specs=P(ROW, COL), check_vma=False
    )
```

```python
import functools

import jax
import jax.numpy as jnp
from jax import lax
from jax.experimental import pallas as pl
from jax.experimental.pallas import tpu as pltpu
from jax.sharding import PartitionSpec as P

LANES = 128
MAIN = 16
EXTRA = 2
PAIR = 2
LIMIT = pltpu.CompilerParams(vmem_limit_bytes=8 * 1024 * 1024)
SCALAR = pl.BlockSpec(memory_space=pltpu.SMEM)
WHOLE = pl.BlockSpec(memory_space=pltpu.VMEM)
SCALE = 16.0
ROW, COL = ("y", "far", "pair"), ("z", "core")
ALONG_X = 4


def lanes(q):
    return slice(q * LANES, (q + 1) * LANES)


def rows_of(q, count):
    return slice(q * count, (q + 1) * count)


def gather_extra(tiles, shift_of):
    row = lax.broadcasted_iota(jnp.int32, tiles[0].shape, 0) // EXTRA
    out = tiles[0] if shift_of(0) % 8 == 0 else pltpu.roll(tiles[0], shift_of(0) % 8, 0)
    for q in range(1, len(tiles)):
        moved = tiles[q]
        if shift_of(q) % 8:
            moved = pltpu.roll(moved, shift_of(q) % 8, 0)
        out = jnp.where(row == q, moved, out)
    return out


def spread_kernel(x_ref, out_ref):
    x = x_ref[...].astype(jnp.float32)
    tiles = x.shape[1] // LANES
    for q in range(tiles):
        for r in range(out_ref.shape[0]):
            out_ref[r, rows_of(q, MAIN), :] = x_ref[:MAIN, lanes(q)]
    tail = jnp.concatenate(
        [x[MAIN:, lanes(q)] for q in range(tiles)], axis=0
    ).astype(jnp.bfloat16)
    for r in range(out_ref.shape[0]):
        out_ref[r, tiles * MAIN :, :] = tail


def spread(x, copies):
    rows = x.shape[0] * x.shape[1] // LANES
    return pl.pallas_call(
        spread_kernel,
        out_shape=jax.ShapeDtypeStruct((copies, rows, LANES), x.dtype),
        in_specs=[WHOLE],
        out_specs=WHOLE,
        compiler_params=LIMIT,
    )(x)


def add_product(source_at, gate_ref, up_ref, base_ref, out_ref, held):
    sources = out_ref.shape[0]
    tiles = held.shape[1] // LANES
    wide_tiles = gate_ref.shape[1] // LANES
    main = sources * MAIN
    shape = (tiles * sources * 8, sources * 8)
    r = lax.broadcasted_iota(jnp.int32, shape, 0)
    c = lax.broadcasted_iota(jnp.int32, shape, 1)
    place = c == r // 8 % sources * 8 + r // (sources * 8) * EXTRA + r % EXTRA
    tails = []
    for n in range(sources):
        block = source_at(n)
        for q in range(tiles):
            held[rows_of(n, MAIN), lanes(q)] = block[rows_of(q, MAIN)]
        tails.append(block[tiles * MAIN :])
    moved = jnp.dot(
        place.astype(jnp.bfloat16),
        jnp.concatenate(tails, axis=0),
        preferred_element_type=jnp.float32,
    ).astype(jnp.bfloat16)
    for q in range(tiles):
        held[main:, lanes(q)] = moved[rows_of(q, sources * 8)]
    row = lax.broadcasted_iota(jnp.int32, (8, LANES), 0) // EXTRA
    x = held[...]
    for first in range(0, wide_tiles, 2):
        count = min(2, wide_tiles - first)
        columns = slice(first * LANES, (first + count) * LANES)
        gate = jnp.dot(x, gate_ref[:, columns], preferred_element_type=jnp.float32)
        up = jnp.dot(x, up_ref[:, columns], preferred_element_type=jnp.float32)
        for n in range(sources):
            end = slice(main + n * 8, main + n * 8 + 8)
            mixed = jnp.where(row == 0, gate[end, lanes(0)], gate[end, lanes(count - 1)])
            mixed = jnp.where(row == 2, up[end, lanes(0)], mixed)
            mixed = jnp.where(row == 3, up[end, lanes(count - 1)], mixed)
            start = 2 * wide_tiles * MAIN + 4 * first
            parts = [(slice(start, start + 8), mixed)]
            for i in range(count):
                at = rows_of(n, MAIN)
                parts.append((rows_of(first + i, MAIN), gate[at, lanes(i)]))
                parts.append((rows_of(wide_tiles + first + i, MAIN), up[at, lanes(i)]))
            for where, value in parts:
                if base_ref is not None:
                    value += base_ref[n, where, :]
                out_ref[n, where, :] = value


def own_kernel(core_ref, own_ref, gate_ref, up_ref, out_ref, held):
    depth = out_ref.shape[0] // PAIR

    def source_at(n):
        return own_ref[n % depth * 2 * PAIR + core_ref[0] * PAIR + n // depth]

    add_product(source_at, gate_ref, up_ref, None, out_ref, held)


def other_kernel(other_ref, gate_ref, up_ref, base_ref, out_ref, held):
    depth = out_ref.shape[0] // PAIR

    def source_at(n):
        return other_ref[n % depth, n // depth]

    add_product(source_at, gate_ref, up_ref, base_ref, out_ref, held)


def up_product(kernel, specs, sources, operands, gate, up, *base):
    wide_tiles = gate.shape[1] // LANES
    rows = 2 * wide_tiles * MAIN + (wide_tiles + 1) // 2 * 8
    held = pltpu.VMEM((sources * (MAIN + 8), gate.shape[0]), jnp.bfloat16)
    return pl.pallas_call(
        kernel,
        out_shape=pltpu.VMEM((sources, rows, LANES), jnp.float32),
        in_specs=specs + [WHOLE] * (2 + len(base)),
        out_specs=WHOLE,
        scratch_shapes=[held],
        compiler_params=LIMIT,
    )(*operands, gate, up, *base)


def activate_kernel(sum_ref, out_ref):
    wide_tiles = out_ref.shape[1] // LANES

    def total(p, rows):
        return sum_ref[p, rows, :] * (1 / SCALE)

    for p in range(PAIR):
        tail_rows = slice(PAIR * MAIN + p * EXTRA, PAIR * MAIN + (p + 1) * EXTRA)
        for j in range(wide_tiles):
            gate = total(p, rows_of(j, MAIN))
            up = total(p, rows_of(wide_tiles + j, MAIN))
            out_ref[rows_of(p, MAIN), lanes(j)] = (
                gate / (1 + jnp.exp(-gate)) * up
            ).astype(jnp.bfloat16)
        for first in range(0, wide_tiles, 2):
            start = 2 * wide_tiles * MAIN + 4 * first
            mixed = total(p, slice(start, start + 8))
            tail = mixed / (1 + jnp.exp(-mixed)) * pltpu.roll(mixed, 2 * EXTRA, 0)
            tail = tail.astype(jnp.bfloat16)
            for i in range(min(2, wide_tiles - first)):
                out_ref[tail_rows, lanes(first + i)] = tail[rows_of(i, EXTRA)]


def activate(total, hidden_width):
    return pl.pallas_call(
        activate_kernel,
        out_shape=jax.ShapeDtypeStruct(
            (PAIR * (MAIN + EXTRA), hidden_width), jnp.bfloat16
        ),
        in_specs=[WHOLE],
        out_specs=WHOLE,
        compiler_params=LIMIT,
    )(total)


def down_kernel(pair_ref, hidden_ref, own_ref, other_ref, out_ref, own, other):
    sources = hidden_ref.shape[0]
    main = sources * MAIN
    first = pair_ref[0] == 0
    for n in range(sources):
        a, b = hidden_ref[n, :MAIN], hidden_ref[n, MAIN : PAIR * MAIN]
        own[rows_of(n, MAIN), :] = jnp.where(first, a, b)
        other[rows_of(n, MAIN), :] = jnp.where(first, b, a)
        tail = hidden_ref[n, PAIR * MAIN :]
        at = slice(main + n * 8, main + n * 8 + PAIR * EXTRA)
        own[at, :] = tail
        other[at, :] = tail
    tiles = own_ref.shape[1] // LANES
    mine = jnp.dot(own[...], own_ref[...], preferred_element_type=jnp.float32)
    theirs = jnp.dot(other[...], other_ref[...], preferred_element_type=jnp.float32)
    for n in range(sources):
        at, end = rows_of(n, MAIN), slice(main + n * 8, main + n * 8 + 8)
        tails = []
        for q in range(tiles):
            out_ref[n, rows_of(q, MAIN), :] = (
                mine[at, lanes(q)] + theirs[at, lanes(q)]
            ).astype(jnp.bfloat16)
            a, b = mine[end, lanes(q)], theirs[end, lanes(q)]
            later = pltpu.roll(jnp.where(first, b, a), 8 - EXTRA, 0)
            tails.append(jnp.where(first, a, b) + later)
        tail = gather_extra(tails, lambda q: q * EXTRA)
        out_ref[n, tiles * MAIN :, :] = tail.astype(jnp.bfloat16)


def down_product(pair, hidden, weight, other_weight):
    sources, count, width = hidden.shape
    rows = (MAIN + EXTRA) * weight.shape[1] // LANES
    held = pltpu.VMEM((sources * (MAIN + 8), width), jnp.bfloat16)
    return pl.pallas_call(
        down_kernel,
        out_shape=jax.ShapeDtypeStruct((sources, rows, LANES), jnp.bfloat16),
        in_specs=[SCALAR] + [WHOLE] * 3,
        out_specs=WHOLE,
        scratch_shapes=[held, held],
        compiler_params=LIMIT,
    )(pair, hidden, weight, other_weight)


def finish_kernel(shares_ref, out_ref):
    tiles = out_ref.shape[1] // LANES
    total = shares_ref[0].astype(jnp.float32)
    for r in range(1, shares_ref.shape[0]):
        total += shares_ref[r].astype(jnp.float32)
    for q in range(tiles):
        out_ref[:MAIN, lanes(q)] = total[rows_of(q, MAIN)].astype(jnp.bfloat16)
        tail = total[tiles * MAIN + q * EXTRA : tiles * MAIN + (q + 1) * EXTRA]
        out_ref[MAIN:, lanes(q)] = tail.astype(jnp.bfloat16)


def finish(shares):
    width = shares.shape[1] // (MAIN + EXTRA) * LANES
    return pl.pallas_call(
        finish_kernel,
        out_shape=jax.ShapeDtypeStruct((MAIN + EXTRA, width), jnp.bfloat16),
        in_specs=[WHOLE],
        out_specs=WHOLE,
        compiler_params=LIMIT,
    )(shares)


def shards(activations, gate_matrix, up_matrix, down_matrix):
    n_row, depth = lax.axis_size(ROW), lax.axis_size("z")
    core, pair = lax.axis_index("core"), lax.axis_index("pair")

    def swap(x, axis):
        return lax.ppermute(x, axis, [(0, 1), (1, 0)])

    own = lax.all_to_all(spread(activations, n_row), ROW, 0, 0, tiled=True)
    gate_other, up_other = swap(gate_matrix, "core"), swap(up_matrix, "core")
    down_other = swap(down_matrix, "pair")
    by_core = own.reshape(depth, 2, PAIR, *own.shape[1:])
    give = lax.dynamic_index_in_dim(by_core, 1 - core, 1, keepdims=False)
    other = swap(give, "core")
    sources = PAIR * depth
    terms = up_product(
        own_kernel,
        [SCALAR, WHOLE],
        sources,
        (core.reshape(1), own),
        gate_matrix,
        up_matrix,
    )
    terms = up_product(
        other_kernel, [WHOLE], sources, (other,), gate_other, up_other, terms
    )
    arrived = lax.all_to_all(
        (terms * SCALE).astype(jnp.float16), ("pair", "z"), 0, 0, tiled=True
    )
    arrived = arrived.reshape(PAIR, depth, *arrived.shape[1:])
    total = jnp.sum(arrived.astype(jnp.float32), axis=1)
    hidden = activate(total, gate_matrix.shape[1])
    gathered = lax.all_gather(hidden, COL, axis=0, tiled=False)
    share = down_product(pair.reshape(1), gathered, down_matrix, down_other)
    return finish(lax.all_to_all(share, ("y", "far"), 0, 0, tiled=True))


def solution(mesh):
    n_row, n_col = mesh.devices.shape
    far = ALONG_X // PAIR
    devices = mesh.devices.reshape(n_row // ALONG_X, far, PAIR, n_col // 2, 2)
    chips = jax.sharding.Mesh(devices, ROW + COL)
    placed = (P(ROW, COL), P(COL, ROW), P(COL, ROW), P(ROW, COL))
    return jax.shard_map(
        shards, mesh=chips, in_specs=placed, out_specs=P(ROW, COL), check_vma=False
    )
```

```python
import functools

import jax
import jax.numpy as jnp
from jax import lax
from jax.experimental import pallas as pl
from jax.experimental.pallas import tpu as pltpu
from jax.sharding import PartitionSpec as P

LANES = 128
MAIN = 16
EXTRA = 2
PAIR = 2
LIMIT = pltpu.CompilerParams(vmem_limit_bytes=8 * 1024 * 1024)
SCALAR = pl.BlockSpec(memory_space=pltpu.SMEM)
WHOLE = pl.BlockSpec(memory_space=pltpu.VMEM)
SCALE = 16.0
COST = 8
ROW, COL = ("y", "far", "pair"), ("z", "core")
ALONG_X = 4
FAR = ALONG_X // PAIR


def lanes(q):
    return slice(q * LANES, (q + 1) * LANES)


def rows_of(q, count):
    return slice(q * count, (q + 1) * count)


def gather_extra(tiles, shift_of):
    row = lax.broadcasted_iota(jnp.int32, tiles[0].shape, 0) // EXTRA
    out = tiles[0] if shift_of(0) % 8 == 0 else pltpu.roll(tiles[0], shift_of(0) % 8, 0)
    for q in range(1, len(tiles)):
        moved = tiles[q]
        if shift_of(q) % 8:
            moved = pltpu.roll(moved, shift_of(q) % 8, 0)
        out = jnp.where(row == q, moved, out)
    return out


def spread_kernel(x_ref, out_ref):
    x = x_ref[...].astype(jnp.float32)
    tiles = x.shape[1] // LANES
    for q in range(tiles):
        for r in range(out_ref.shape[0]):
            out_ref[r, rows_of(q, MAIN), :] = x_ref[:MAIN, lanes(q)]
    tail = jnp.concatenate(
        [x[MAIN:, lanes(q)] for q in range(tiles)], axis=0
    ).astype(jnp.bfloat16)
    for r in range(out_ref.shape[0]):
        out_ref[r, tiles * MAIN :, :] = tail


def spread(x, copies):
    rows = x.shape[0] * x.shape[1] // LANES
    return pl.pallas_call(
        spread_kernel,
        out_shape=jax.ShapeDtypeStruct((copies, rows, LANES), x.dtype),
        in_specs=[WHOLE],
        out_specs=WHOLE,
        compiler_params=LIMIT,
    )(x)


def add_product(source_at, gate_ref, up_ref, base_ref, out_ref, held):
    sources = out_ref.shape[0]
    tiles = held.shape[1] // LANES
    wide_tiles = gate_ref.shape[1] // LANES
    main = sources * MAIN
    shape = (tiles * sources * 8, sources * 8)
    r = lax.broadcasted_iota(jnp.int32, shape, 0)
    c = lax.broadcasted_iota(jnp.int32, shape, 1)
    place = c == r // 8 % sources * 8 + r // (sources * 8) * EXTRA + r % EXTRA
    tails = []
    for n in range(sources):
        block = source_at(n)
        for q in range(tiles):
            held[rows_of(n, MAIN), lanes(q)] = block[rows_of(q, MAIN)]
        tails.append(block[tiles * MAIN :])
    moved = jnp.dot(
        place.astype(jnp.bfloat16),
        jnp.concatenate(tails, axis=0),
        preferred_element_type=jnp.float32,
    ).astype(jnp.bfloat16)
    for q in range(tiles):
        held[main:, lanes(q)] = moved[rows_of(q, sources * 8)]
    row = lax.broadcasted_iota(jnp.int32, (8, LANES), 0) // EXTRA
    x = held[...]
    for first in range(0, wide_tiles, 2):
        count = min(2, wide_tiles - first)
        columns = slice(first * LANES, (first + count) * LANES)
        gate = jnp.dot(x, gate_ref[:, columns], preferred_element_type=jnp.float32)
        up = jnp.dot(x, up_ref[:, columns], preferred_element_type=jnp.float32)
        for n in range(sources):
            end = slice(main + n * 8, main + n * 8 + 8)
            mixed = jnp.where(row == 0, gate[end, lanes(0)], gate[end, lanes(count - 1)])
            mixed = jnp.where(row == 2, up[end, lanes(0)], mixed)
            mixed = jnp.where(row == 3, up[end, lanes(count - 1)], mixed)
            start = 2 * wide_tiles * MAIN + 4 * first
            parts = [(slice(start, start + 8), mixed)]
            for i in range(count):
                at = rows_of(n, MAIN)
                parts.append((rows_of(first + i, MAIN), gate[at, lanes(i)]))
                parts.append((rows_of(wide_tiles + first + i, MAIN), up[at, lanes(i)]))
            for where, value in parts:
                if base_ref is not None:
                    value += base_ref[n, where, :]
                out_ref[n, where, :] = value


def up_kernel(flip, core_ref, got_ref, gate_ref, up_ref, *refs):
    *base, out_ref, held = refs
    depth = out_ref.shape[0] // PAIR
    side = flip + (1 - 2 * flip) * core_ref[0]

    def source_at(n):
        b = n % depth
        return got_ref[(b % FAR * PAIR + n // depth) * 2 + side, b // FAR]

    add_product(source_at, gate_ref, up_ref, base[0] if base else None, out_ref, held)


def up_product(flip, core, got, sources, gate, up, *base):
    wide_tiles = gate.shape[1] // LANES
    rows = 2 * wide_tiles * MAIN + (wide_tiles + 1) // 2 * 8
    held = pltpu.VMEM((sources * (MAIN + 8), gate.shape[0]), jnp.bfloat16)
    work = COST * sources * (MAIN + 8) * gate.size
    return pl.pallas_call(
        functools.partial(up_kernel, flip),
        cost_estimate=pl.CostEstimate(
            flops=4 * work, bytes_accessed=4 * gate.size, transcendentals=0
        ),
        out_shape=pltpu.VMEM((sources, rows, LANES), jnp.float32),
        in_specs=[SCALAR] + [WHOLE] * (3 + len(base)),
        out_specs=WHOLE,
        scratch_shapes=[held],
        compiler_params=LIMIT,
    )(core, got, gate, up, *base)


def activate_kernel(sum_ref, out_ref):
    wide_tiles = out_ref.shape[1] // LANES

    def total(p, rows):
        return sum_ref[p, rows, :] * (1 / SCALE)

    for p in range(PAIR):
        tail_rows = slice(PAIR * MAIN + p * EXTRA, PAIR * MAIN + (p + 1) * EXTRA)
        for j in range(wide_tiles):
            gate = total(p, rows_of(j, MAIN))
            up = total(p, rows_of(wide_tiles + j, MAIN))
            out_ref[rows_of(p, MAIN), lanes(j)] = (
                gate / (1 + jnp.exp(-gate)) * up
            ).astype(jnp.bfloat16)
        for first in range(0, wide_tiles, 2):
            start = 2 * wide_tiles * MAIN + 4 * first
            mixed = total(p, slice(start, start + 8))
            tail = mixed / (1 + jnp.exp(-mixed)) * pltpu.roll(mixed, 2 * EXTRA, 0)
            tail = tail.astype(jnp.bfloat16)
            for i in range(min(2, wide_tiles - first)):
                out_ref[tail_rows, lanes(first + i)] = tail[rows_of(i, EXTRA)]


def activate(total, hidden_width):
    return pl.pallas_call(
        activate_kernel,
        out_shape=jax.ShapeDtypeStruct(
            (PAIR * (MAIN + EXTRA), hidden_width), jnp.bfloat16
        ),
        in_specs=[WHOLE],
        out_specs=WHOLE,
        compiler_params=LIMIT,
    )(total)


def down_kernel(pair_ref, hidden_ref, own_ref, other_ref, out_ref, own, other):
    sources = hidden_ref.shape[0]
    main = sources * MAIN
    first = pair_ref[0] == 0
    for n in range(sources):
        a, b = hidden_ref[n, :MAIN], hidden_ref[n, MAIN : PAIR * MAIN]
        own[rows_of(n, MAIN), :] = jnp.where(first, a, b)
        other[rows_of(n, MAIN), :] = jnp.where(first, b, a)
        tail = hidden_ref[n, PAIR * MAIN :]
        at = slice(main + n * 8, main + n * 8 + PAIR * EXTRA)
        own[at, :] = tail
        other[at, :] = tail
    tiles = own_ref.shape[1] // LANES
    mine = jnp.dot(own[...], own_ref[...], preferred_element_type=jnp.float32)
    theirs = jnp.dot(other[...], other_ref[...], preferred_element_type=jnp.float32)
    for n in range(sources):
        at, end = rows_of(n, MAIN), slice(main + n * 8, main + n * 8 + 8)
        to = n % 2 * (sources // 2) + n // 2
        tails = []
        for q in range(tiles):
            out_ref[to, rows_of(q, MAIN), :] = (
                mine[at, lanes(q)] + theirs[at, lanes(q)]
            ).astype(jnp.bfloat16)
            a, b = mine[end, lanes(q)], theirs[end, lanes(q)]
            later = pltpu.roll(jnp.where(first, b, a), 8 - EXTRA, 0)
            tails.append(jnp.where(first, a, b) + later)
        tail = gather_extra(tails, lambda q: q * EXTRA)
        out_ref[to, tiles * MAIN :, :] = tail.astype(jnp.bfloat16)


def down_product(pair, hidden, weight, other_weight):
    sources, count, width = hidden.shape
    rows = (MAIN + EXTRA) * weight.shape[1] // LANES
    held = pltpu.VMEM((sources * (MAIN + 8), width), jnp.bfloat16)
    return pl.pallas_call(
        down_kernel,
        out_shape=jax.ShapeDtypeStruct((sources, rows, LANES), jnp.bfloat16),
        in_specs=[SCALAR] + [WHOLE] * 3,
        out_specs=WHOLE,
        scratch_shapes=[held, held],
        compiler_params=LIMIT,
    )(pair, hidden, weight, other_weight)


def finish_kernel(shares_ref, out_ref):
    tiles = out_ref.shape[1] // LANES
    total = shares_ref[0].astype(jnp.float32)
    for r in range(1, shares_ref.shape[0]):
        total += shares_ref[r].astype(jnp.float32)
    for q in range(tiles):
        out_ref[:MAIN, lanes(q)] = total[rows_of(q, MAIN)].astype(jnp.bfloat16)
        tail = total[tiles * MAIN + q * EXTRA : tiles * MAIN + (q + 1) * EXTRA]
        out_ref[MAIN:, lanes(q)] = tail.astype(jnp.bfloat16)


def finish(shares):
    width = shares.shape[1] // (MAIN + EXTRA) * LANES
    return pl.pallas_call(
        finish_kernel,
        out_shape=jax.ShapeDtypeStruct((MAIN + EXTRA, width), jnp.bfloat16),
        in_specs=[WHOLE],
        out_specs=WHOLE,
        compiler_params=LIMIT,
    )(shares)


def shards(activations, gate_matrix, up_matrix, down_matrix):
    n_row, depth = lax.axis_size(ROW), lax.axis_size("z")
    core, pair = lax.axis_index("core"), lax.axis_index("pair")

    def swap(x, axis):
        return lax.ppermute(x, axis, [(0, 1), (1, 0)])

    near = lax.all_to_all(
        spread(activations, n_row // ALONG_X), "y", 0, 0, tiled=True
    )
    halves = near.reshape(1, 2, near.shape[0] // 2, *near.shape[1:])
    halves = jnp.broadcast_to(halves, (ALONG_X, *halves.shape[1:]))
    halves = halves.reshape(2 * ALONG_X, *halves.shape[2:])
    halves, gate, up = lax.optimization_barrier((halves, gate_matrix, up_matrix))
    gate_other, up_other = swap(gate, "core"), swap(up, "core")
    down_other = swap(down_matrix, "pair")
    got = lax.all_to_all(
        halves,
        ("far", "pair", "core"),
        0,
        0,
        tiled=True,
    )
    me, sources = core.reshape(1), PAIR * depth
    terms = up_product(0, me, got, sources, gate, up)
    terms = up_product(1, me, got, sources, gate_other, up_other, terms)
    arrived = lax.all_to_all(
        (terms * SCALE).astype(jnp.float16), ("pair", "z"), 0, 0, tiled=True
    )
    arrived = arrived.reshape(PAIR, depth, *arrived.shape[1:])
    total = jnp.sum(arrived.astype(jnp.float32), axis=1)
    hidden = activate(total, gate_matrix.shape[1])
    gathered = lax.all_gather(hidden, COL, axis=0, tiled=False)
    share = down_product(pair.reshape(1), gathered, down_matrix, down_other)
    return finish(lax.all_to_all(share, ("y", "far"), 0, 0, tiled=True))


def solution(mesh):
    n_row, n_col = mesh.devices.shape
    devices = mesh.devices.reshape(n_row // ALONG_X, FAR, PAIR, n_col // 2, 2)
    chips = jax.sharding.Mesh(devices, ROW + COL)
    placed = (P(ROW, COL), P(COL, ROW), P(COL, ROW), P(ROW, COL))
    return jax.shard_map(
        shards, mesh=chips, in_specs=placed, out_specs=P(ROW, COL), check_vma=False
    )
```

```python
import functools

import jax
import jax.numpy as jnp
from jax import lax
from jax.experimental import pallas as pl
from jax.experimental.pallas import tpu as pltpu
from jax.sharding import PartitionSpec as P

LANES = 128
MAIN = 16
EXTRA = 2
PAIR = 2
LIMIT = pltpu.CompilerParams(vmem_limit_bytes=8 * 1024 * 1024)
SCALAR = pl.BlockSpec(memory_space=pltpu.SMEM)
WHOLE = pl.BlockSpec(memory_space=pltpu.VMEM)
SCALE = 16.0
COST = 8
ROW, COL = ("y", "far", "pair"), ("z", "core")
ALONG_X = 4
FAR = ALONG_X // PAIR


def lanes(q):
    return slice(q * LANES, (q + 1) * LANES)


def rows_of(q, count):
    return slice(q * count, (q + 1) * count)


def gather_extra(tiles, shift_of):
    row = lax.broadcasted_iota(jnp.int32, tiles[0].shape, 0) // EXTRA
    out = tiles[0] if shift_of(0) % 8 == 0 else pltpu.roll(tiles[0], shift_of(0) % 8, 0)
    for q in range(1, len(tiles)):
        moved = tiles[q]
        if shift_of(q) % 8:
            moved = pltpu.roll(moved, shift_of(q) % 8, 0)
        out = jnp.where(row == q, moved, out)
    return out


def spread_kernel(x_ref, out_ref):
    x = x_ref[...].astype(jnp.float32)
    tiles = x.shape[1] // LANES
    for q in range(tiles):
        for r in range(out_ref.shape[0]):
            out_ref[r, rows_of(q, MAIN), :] = x_ref[:MAIN, lanes(q)]
    tail = jnp.concatenate(
        [x[MAIN:, lanes(q)] for q in range(tiles)], axis=0
    ).astype(jnp.bfloat16)
    for r in range(out_ref.shape[0]):
        out_ref[r, tiles * MAIN :, :] = tail


def spread(x, copies):
    rows = x.shape[0] * x.shape[1] // LANES
    return pl.pallas_call(
        spread_kernel,
        out_shape=jax.ShapeDtypeStruct((copies, rows, LANES), x.dtype),
        in_specs=[WHOLE],
        out_specs=WHOLE,
        compiler_params=LIMIT,
    )(x)


def add_product(source_at, ready, gate_ref, up_ref, base_ref, out_ref, held):
    sources = out_ref.shape[0]
    tiles = held.shape[1] // LANES
    wide_tiles = gate_ref.shape[1] // LANES
    main = sources * MAIN
    shape = (tiles * sources * 8, sources * 8)
    r = lax.broadcasted_iota(jnp.int32, shape, 0)
    c = lax.broadcasted_iota(jnp.int32, shape, 1)
    place = c == r // 8 % sources * 8 + r // (sources * 8) * EXTRA + r % EXTRA
    tails = []
    for n in range(sources):
        block = source_at(n)
        for q in range(tiles):
            held[rows_of(n, MAIN), lanes(q)] = block[rows_of(q, MAIN)]
        tails.append(block[tiles * MAIN :])
    moved = jnp.dot(
        place.astype(jnp.bfloat16),
        jnp.concatenate(tails, axis=0),
        preferred_element_type=jnp.float32,
    ).astype(jnp.bfloat16)
    for q in range(tiles):
        held[main:, lanes(q)] = moved[rows_of(q, sources * 8)]
    row = lax.broadcasted_iota(jnp.int32, (8, LANES), 0) // EXTRA
    x = held[...]
    for kind, weight_ref in enumerate((gate_ref, up_ref)):
        if kind:
            ready()
        for first in range(0, wide_tiles, 2):
            count = min(2, wide_tiles - first)
            columns = slice(first * LANES, (first + count) * LANES)
            term = jnp.dot(x, weight_ref[:, columns], preferred_element_type=jnp.float32)
            for n in range(sources):
                end = slice(main + n * 8, main + n * 8 + 8)
                start = 2 * wide_tiles * MAIN + 4 * first
                where = slice(start, start + 8)
                mixed = jnp.where(
                    row % 2 == 0, term[end, lanes(0)], term[end, lanes(count - 1)]
                )
                if base_ref is not None:
                    mixed += base_ref[n, where, :]
                if kind:
                    mixed = jnp.where(row < 2, out_ref[n, where, :], mixed)
                out_ref[n, where, :] = mixed
                for i in range(count):
                    where = rows_of(kind * wide_tiles + first + i, MAIN)
                    value = term[rows_of(n, MAIN), lanes(i)]
                    if base_ref is not None:
                        value += base_ref[n, where, :]
                    out_ref[n, where, :] = value


def up_kernel(flip, core_ref, got_ref, gate_ref, up_ref, *refs):
    base_ref, ready = None, lambda: None
    if flip:
        base_ref, out_ref, held, up_held, done = refs
        fetch = pltpu.make_async_copy(up_ref, up_held, done)
        fetch.start()
        up_ref, ready = up_held, fetch.wait
    else:
        out_ref, held = refs
    depth = out_ref.shape[0] // PAIR
    side = flip + (1 - 2 * flip) * core_ref[0]

    def source_at(n):
        b = n % depth
        return got_ref[(b % FAR * PAIR + n // depth) * 2 + side, b // FAR]

    add_product(source_at, ready, gate_ref, up_ref, base_ref, out_ref, held)


def up_product(flip, core, got, sources, gate, up, *base):
    wide_tiles = gate.shape[1] // LANES
    rows = 2 * wide_tiles * MAIN + (wide_tiles + 1) // 2 * 8
    work = COST * sources * (MAIN + 8) * gate.size
    held = [pltpu.VMEM((sources * (MAIN + 8), gate.shape[0]), jnp.bfloat16)]
    up_spec = WHOLE
    if flip:
        held += [pltpu.VMEM(up.shape, up.dtype), pltpu.SemaphoreType.DMA]
        up_spec = pl.BlockSpec(memory_space=pl.ANY)
    return pl.pallas_call(
        functools.partial(up_kernel, flip),
        cost_estimate=pl.CostEstimate(
            flops=4 * work, bytes_accessed=4 * gate.size, transcendentals=0
        ),
        out_shape=pltpu.VMEM((sources, rows, LANES), jnp.float32),
        in_specs=[SCALAR, WHOLE, WHOLE, up_spec] + [WHOLE] * len(base),
        out_specs=WHOLE,
        scratch_shapes=held,
        compiler_params=LIMIT,
    )(core, got, gate, up, *base)


def activate_kernel(sum_ref, out_ref):
    wide_tiles = out_ref.shape[1] // LANES

    def total(p, rows):
        return sum_ref[p, rows, :] * (1 / SCALE)

    for p in range(PAIR):
        tail_rows = slice(PAIR * MAIN + p * EXTRA, PAIR * MAIN + (p + 1) * EXTRA)
        for j in range(wide_tiles):
            gate = total(p, rows_of(j, MAIN))
            up = total(p, rows_of(wide_tiles + j, MAIN))
            out_ref[rows_of(p, MAIN), lanes(j)] = (
                gate / (1 + jnp.exp(-gate)) * up
            ).astype(jnp.bfloat16)
        for first in range(0, wide_tiles, 2):
            start = 2 * wide_tiles * MAIN + 4 * first
            mixed = total(p, slice(start, start + 8))
            tail = mixed / (1 + jnp.exp(-mixed)) * pltpu.roll(mixed, 2 * EXTRA, 0)
            tail = tail.astype(jnp.bfloat16)
            for i in range(min(2, wide_tiles - first)):
                out_ref[tail_rows, lanes(first + i)] = tail[rows_of(i, EXTRA)]


def activate(total, hidden_width):
    return pl.pallas_call(
        activate_kernel,
        out_shape=jax.ShapeDtypeStruct(
            (PAIR * (MAIN + EXTRA), hidden_width), jnp.bfloat16
        ),
        in_specs=[WHOLE],
        out_specs=WHOLE,
        compiler_params=LIMIT,
    )(total)


def down_kernel(pair_ref, hidden_ref, own_ref, other_ref, out_ref, own, other):
    sources = hidden_ref.shape[0]
    main = sources * MAIN
    first = pair_ref[0] == 0
    for n in range(sources):
        a, b = hidden_ref[n, :MAIN], hidden_ref[n, MAIN : PAIR * MAIN]
        own[rows_of(n, MAIN), :] = jnp.where(first, a, b)
        other[rows_of(n, MAIN), :] = jnp.where(first, b, a)
        tail = hidden_ref[n, PAIR * MAIN :]
        at = slice(main + n * 8, main + n * 8 + PAIR * EXTRA)
        own[at, :] = tail
        other[at, :] = tail
    tiles = own_ref.shape[1] // LANES
    mine = jnp.dot(own[...], own_ref[...], preferred_element_type=jnp.float32)
    theirs = jnp.dot(other[...], other_ref[...], preferred_element_type=jnp.float32)
    for n in range(sources):
        at, end = rows_of(n, MAIN), slice(main + n * 8, main + n * 8 + 8)
        to = n % 2 * (sources // 2) + n // 2
        tails = []
        for q in range(tiles):
            out_ref[to, rows_of(q, MAIN), :] = (
                mine[at, lanes(q)] + theirs[at, lanes(q)]
            ).astype(jnp.bfloat16)
            a, b = mine[end, lanes(q)], theirs[end, lanes(q)]
            later = pltpu.roll(jnp.where(first, b, a), 8 - EXTRA, 0)
            tails.append(jnp.where(first, a, b) + later)
        tail = gather_extra(tails, lambda q: q * EXTRA)
        out_ref[to, tiles * MAIN :, :] = tail.astype(jnp.bfloat16)


def down_product(pair, hidden, weight, other_weight):
    sources, count, width = hidden.shape
    rows = (MAIN + EXTRA) * weight.shape[1] // LANES
    held = pltpu.VMEM((sources * (MAIN + 8), width), jnp.bfloat16)
    return pl.pallas_call(
        down_kernel,
        out_shape=jax.ShapeDtypeStruct((sources, rows, LANES), jnp.bfloat16),
        in_specs=[SCALAR] + [WHOLE] * 3,
        out_specs=WHOLE,
        scratch_shapes=[held, held],
        compiler_params=LIMIT,
    )(pair, hidden, weight, other_weight)


def finish_kernel(shares_ref, out_ref):
    tiles = out_ref.shape[1] // LANES
    total = shares_ref[0].astype(jnp.float32)
    for r in range(1, shares_ref.shape[0]):
        total += shares_ref[r].astype(jnp.float32)
    for q in range(tiles):
        out_ref[:MAIN, lanes(q)] = total[rows_of(q, MAIN)].astype(jnp.bfloat16)
        tail = total[tiles * MAIN + q * EXTRA : tiles * MAIN + (q + 1) * EXTRA]
        out_ref[MAIN:, lanes(q)] = tail.astype(jnp.bfloat16)


def finish(shares):
    width = shares.shape[1] // (MAIN + EXTRA) * LANES
    return pl.pallas_call(
        finish_kernel,
        out_shape=jax.ShapeDtypeStruct((MAIN + EXTRA, width), jnp.bfloat16),
        in_specs=[WHOLE],
        out_specs=WHOLE,
        compiler_params=LIMIT,
    )(shares)


def shards(activations, gate_matrix, up_matrix, down_matrix):
    n_row, depth = lax.axis_size(ROW), lax.axis_size("z")
    core, pair = lax.axis_index("core"), lax.axis_index("pair")

    def swap(x, axis):
        return lax.ppermute(x, axis, [(0, 1), (1, 0)])

    near = lax.all_to_all(
        spread(activations, n_row // ALONG_X), "y", 0, 0, tiled=True
    )
    halves = near.reshape(1, 2, near.shape[0] // 2, *near.shape[1:])
    halves = jnp.broadcast_to(halves, (ALONG_X, *halves.shape[1:]))
    halves = halves.reshape(2 * ALONG_X, *halves.shape[2:])
    halves, gate, up = lax.optimization_barrier((halves, gate_matrix, up_matrix))
    gate_other, up_other = swap(gate, "core"), swap(up, "core")
    down_other = swap(down_matrix, "pair")
    got = lax.all_to_all(
        halves,
        ("far", "pair", "core"),
        0,
        0,
        tiled=True,
    )
    me, sources = core.reshape(1), PAIR * depth
    terms = up_product(0, me, got, sources, gate, up)
    terms = up_product(1, me, got, sources, gate_other, up_other, terms)
    arrived = lax.all_to_all(
        (terms * SCALE).astype(jnp.float16), ("pair", "z"), 0, 0, tiled=True
    )
    arrived = arrived.reshape(PAIR, depth, *arrived.shape[1:])
    total = jnp.sum(arrived.astype(jnp.float32), axis=1)
    hidden = activate(total, gate_matrix.shape[1])
    gathered = lax.all_gather(hidden, COL, axis=0, tiled=False)
    share = down_product(pair.reshape(1), gathered, down_matrix, down_other)
    return finish(lax.all_to_all(share, ("y", "far"), 0, 0, tiled=True))


def solution(mesh):
    n_row, n_col = mesh.devices.shape
    devices = mesh.devices.reshape(n_row // ALONG_X, FAR, PAIR, n_col // 2, 2)
    chips = jax.sharding.Mesh(devices, ROW + COL)
    placed = (P(ROW, COL), P(COL, ROW), P(COL, ROW), P(ROW, COL))
    return jax.shard_map(
        shards, mesh=chips, in_specs=placed, out_specs=P(ROW, COL), check_vma=False
    )
```

```python
import functools

import jax
import jax.numpy as jnp
from jax import lax
from jax.experimental import pallas as pl
from jax.experimental.pallas import tpu as pltpu
from jax.sharding import PartitionSpec as P

LANES = 128
MAIN = 16
EXTRA = 2
PAIR = 2
LIMIT = pltpu.CompilerParams(vmem_limit_bytes=8 * 1024 * 1024)
SCALAR = pl.BlockSpec(memory_space=pltpu.SMEM)
WHOLE = pl.BlockSpec(memory_space=pltpu.VMEM)
SCALE = 16.0
COST = 8
ROW, COL = ("y", "far", "pair"), ("z", "core")
ALONG_X = 4
FAR = ALONG_X // PAIR


def lanes(q):
    return slice(q * LANES, (q + 1) * LANES)


def rows_of(q, count):
    return slice(q * count, (q + 1) * count)


def gather_extra(tiles, shift_of):
    row = lax.broadcasted_iota(jnp.int32, tiles[0].shape, 0) // EXTRA
    out = tiles[0] if shift_of(0) % 8 == 0 else pltpu.roll(tiles[0], shift_of(0) % 8, 0)
    for q in range(1, len(tiles)):
        moved = tiles[q]
        if shift_of(q) % 8:
            moved = pltpu.roll(moved, shift_of(q) % 8, 0)
        out = jnp.where(row == q, moved, out)
    return out


def spread_kernel(x_ref, out_ref):
    x = x_ref[...].astype(jnp.float32)
    tiles = x.shape[1] // LANES
    for q in range(tiles):
        for r in range(out_ref.shape[0]):
            out_ref[r, rows_of(q, MAIN), :] = x_ref[:MAIN, lanes(q)]
    tail = jnp.concatenate(
        [x[MAIN:, lanes(q)] for q in range(tiles)], axis=0
    ).astype(jnp.bfloat16)
    for r in range(out_ref.shape[0]):
        out_ref[r, tiles * MAIN :, :] = tail


def spread(x, copies):
    rows = x.shape[0] * x.shape[1] // LANES
    return pl.pallas_call(
        spread_kernel,
        out_shape=jax.ShapeDtypeStruct((copies, rows, LANES), x.dtype),
        in_specs=[WHOLE],
        out_specs=WHOLE,
        compiler_params=LIMIT,
    )(x)


def add_product(source_at, ready, gate_ref, up_ref, base_ref, out_ref, held):
    sources = out_ref.shape[0]
    tiles = held.shape[1] // LANES
    wide_tiles = gate_ref.shape[1] // LANES
    main = sources * MAIN
    shape = (tiles * sources * 8, sources * 8)
    r = lax.broadcasted_iota(jnp.int32, shape, 0)
    c = lax.broadcasted_iota(jnp.int32, shape, 1)
    place = c == r // 8 % sources * 8 + r // (sources * 8) * EXTRA + r % EXTRA
    tails = []
    for n in range(sources):
        block = source_at(n)
        for q in range(tiles):
            held[rows_of(n, MAIN), lanes(q)] = block[rows_of(q, MAIN)]
        tails.append(block[tiles * MAIN :])
    moved = jnp.dot(
        place.astype(jnp.bfloat16),
        jnp.concatenate(tails, axis=0),
        preferred_element_type=jnp.float32,
    ).astype(jnp.bfloat16)
    for q in range(tiles):
        held[main:, lanes(q)] = moved[rows_of(q, sources * 8)]
    row = lax.broadcasted_iota(jnp.int32, (8, LANES), 0) // EXTRA
    x = held[...]
    for kind, weight_ref in enumerate((gate_ref, up_ref)):
        if kind:
            ready()
        for first in range(0, wide_tiles, 2):
            count = min(2, wide_tiles - first)
            columns = slice(first * LANES, (first + count) * LANES)
            term = jnp.dot(x, weight_ref[:, columns], preferred_element_type=jnp.float32)
            for n in range(sources):
                end = slice(main + n * 8, main + n * 8 + 8)
                start = 2 * wide_tiles * MAIN + 4 * first
                where = slice(start, start + 8)
                mixed = jnp.where(
                    row % 2 == 0, term[end, lanes(0)], term[end, lanes(count - 1)]
                )
                if base_ref is not None:
                    mixed += base_ref[n, where, :]
                if kind:
                    mixed = jnp.where(row < 2, out_ref[n, where, :], mixed)
                out_ref[n, where, :] = mixed
                for i in range(count):
                    where = rows_of(kind * wide_tiles + first + i, MAIN)
                    value = term[rows_of(n, MAIN), lanes(i)]
                    if base_ref is not None:
                        value += base_ref[n, where, :]
                    out_ref[n, where, :] = value


def up_kernel(flip, core_ref, got_ref, gate_ref, up_ref, *refs):
    base_ref, ready = None, lambda: None
    if flip:
        base_ref, out_ref, held, up_held, done = refs
        fetch = pltpu.make_async_copy(up_ref, up_held, done)
        fetch.start()
        up_ref, ready = up_held, fetch.wait
    else:
        out_ref, held = refs
    depth = out_ref.shape[0] // PAIR
    side = flip + (1 - 2 * flip) * core_ref[0]

    def source_at(n):
        b = n % depth
        return got_ref[(b % FAR * PAIR + n // depth) * 2 + side, b // FAR]

    add_product(source_at, ready, gate_ref, up_ref, base_ref, out_ref, held)


def up_product(flip, core, got, sources, gate, up, *base):
    wide_tiles = gate.shape[1] // LANES
    rows = 2 * wide_tiles * MAIN + (wide_tiles + 1) // 2 * 8
    work = COST * sources * (MAIN + 8) * gate.size
    held = [pltpu.VMEM((sources * (MAIN + 8), gate.shape[0]), jnp.bfloat16)]
    up_spec = WHOLE
    if flip:
        held += [pltpu.VMEM(up.shape, up.dtype), pltpu.SemaphoreType.DMA]
        up_spec = pl.BlockSpec(memory_space=pl.ANY)
    return pl.pallas_call(
        functools.partial(up_kernel, flip),
        cost_estimate=pl.CostEstimate(
            flops=4 * work, bytes_accessed=4 * gate.size, transcendentals=0
        ),
        out_shape=pltpu.VMEM((sources, rows, LANES), jnp.float32),
        in_specs=[SCALAR, WHOLE, WHOLE, up_spec] + [WHOLE] * len(base),
        out_specs=WHOLE,
        scratch_shapes=held,
        compiler_params=LIMIT,
    )(core, got, gate, up, *base)


def activate_kernel(sum_ref, out_ref):
    wide_tiles = out_ref.shape[0] // (PAIR * (MAIN + EXTRA))
    row = lax.broadcasted_iota(jnp.int32, (8, LANES), 0) // EXTRA

    def total(p, rows):
        return sum_ref[p, rows, :] * (1 / SCALE)

    for p in range(PAIR):
        for j in range(wide_tiles):
            gate = total(p, rows_of(j, MAIN))
            up = total(p, rows_of(wide_tiles + j, MAIN))
            out_ref[rows_of(j * PAIR + p, MAIN), :] = (
                gate / (1 + jnp.exp(-gate)) * up
            ).astype(jnp.bfloat16)
    for first in range(0, wide_tiles, 2):
        start = 2 * wide_tiles * MAIN + 4 * first
        tails = []
        for p in range(PAIR):
            mixed = total(p, slice(start, start + 8))
            tails.append(mixed / (1 + jnp.exp(-mixed)) * pltpu.roll(mixed, 4, 0))
        low, high = tails
        tail = jnp.where(row == 1, pltpu.roll(high, 2, 0), low)
        tail = jnp.where(row == 2, pltpu.roll(low, 2, 0), tail)
        tail = jnp.where(row == 3, pltpu.roll(high, 4, 0), tail)
        count = min(2, wide_tiles - first) * 4
        start = wide_tiles * PAIR * MAIN + 4 * first
        out_ref[start : start + count, :] = tail[:count].astype(jnp.bfloat16)


def activate(total, hidden_width):
    return pl.pallas_call(
        activate_kernel,
        out_shape=jax.ShapeDtypeStruct(
            (PAIR * (MAIN + EXTRA) * hidden_width // LANES, LANES), jnp.bfloat16
        ),
        in_specs=[WHOLE],
        out_specs=WHOLE,
        compiler_params=LIMIT,
    )(total)


def down_kernel(pair_ref, hidden_ref, own_ref, other_ref, out_ref, own, other):
    sources = hidden_ref.shape[0]
    main = sources * MAIN
    first = pair_ref[0] == 0
    wide_tiles = own.shape[1] // LANES
    for n in range(sources):
        for j in range(wide_tiles):
            a = hidden_ref[n, rows_of(j * PAIR, MAIN), :]
            b = hidden_ref[n, rows_of(j * PAIR + 1, MAIN), :]
            own[rows_of(n, MAIN), lanes(j)] = jnp.where(first, a, b)
            other[rows_of(n, MAIN), lanes(j)] = jnp.where(first, b, a)
        for j in range(0, wide_tiles, 2):
            count = min(2, wide_tiles - j)
            start = wide_tiles * PAIR * MAIN + 4 * j
            tail = hidden_ref[n, start : start + 4 * count, :]
            at = slice(main + n * 8, main + n * 8 + 4 * count)
            own[at, lanes(j)] = tail
            other[at, lanes(j)] = tail
            if count == 2:
                tail = pltpu.roll(tail.astype(jnp.float32), 4, 0).astype(jnp.bfloat16)
                own[at, lanes(j + 1)] = tail
                other[at, lanes(j + 1)] = tail
    tiles = own_ref.shape[1] // LANES
    mine = jnp.dot(own[...], own_ref[...], preferred_element_type=jnp.float32)
    theirs = jnp.dot(other[...], other_ref[...], preferred_element_type=jnp.float32)
    for n in range(sources):
        at, end = rows_of(n, MAIN), slice(main + n * 8, main + n * 8 + 8)
        to = n % 2 * (sources // 2) + n // 2
        tails = []
        for q in range(tiles):
            out_ref[to, rows_of(q, MAIN), :] = (
                mine[at, lanes(q)] + theirs[at, lanes(q)]
            ).astype(jnp.bfloat16)
            a, b = mine[end, lanes(q)], theirs[end, lanes(q)]
            later = pltpu.roll(jnp.where(first, b, a), 8 - EXTRA, 0)
            tails.append(jnp.where(first, a, b) + later)
        tail = gather_extra(tails, lambda q: q * EXTRA)
        out_ref[to, tiles * MAIN :, :] = tail.astype(jnp.bfloat16)


def down_product(pair, hidden, weight, other_weight):
    sources, width = hidden.shape[0], weight.shape[0]
    rows = (MAIN + EXTRA) * weight.shape[1] // LANES
    held = pltpu.VMEM((sources * (MAIN + 8), width), jnp.bfloat16)
    return pl.pallas_call(
        down_kernel,
        out_shape=jax.ShapeDtypeStruct((sources, rows, LANES), jnp.bfloat16),
        in_specs=[SCALAR] + [WHOLE] * 3,
        out_specs=WHOLE,
        scratch_shapes=[held, held],
        compiler_params=LIMIT,
    )(pair, hidden, weight, other_weight)


def finish_kernel(shares_ref, out_ref):
    tiles = out_ref.shape[1] // LANES
    total = shares_ref[0].astype(jnp.float32)
    for r in range(1, shares_ref.shape[0]):
        total += shares_ref[r].astype(jnp.float32)
    for q in range(tiles):
        out_ref[:MAIN, lanes(q)] = total[rows_of(q, MAIN)].astype(jnp.bfloat16)
        tail = total[tiles * MAIN + q * EXTRA : tiles * MAIN + (q + 1) * EXTRA]
        out_ref[MAIN:, lanes(q)] = tail.astype(jnp.bfloat16)


def finish(shares):
    width = shares.shape[1] // (MAIN + EXTRA) * LANES
    return pl.pallas_call(
        finish_kernel,
        out_shape=jax.ShapeDtypeStruct((MAIN + EXTRA, width), jnp.bfloat16),
        in_specs=[WHOLE],
        out_specs=WHOLE,
        compiler_params=LIMIT,
    )(shares)


def shards(activations, gate_matrix, up_matrix, down_matrix):
    n_row, depth = lax.axis_size(ROW), lax.axis_size("z")
    core, pair = lax.axis_index("core"), lax.axis_index("pair")

    def swap(x, axis):
        return lax.ppermute(x, axis, [(0, 1), (1, 0)])

    near = lax.all_to_all(
        spread(activations, n_row // ALONG_X), "y", 0, 0, tiled=True
    )
    halves = near.reshape(1, 2, near.shape[0] // 2, *near.shape[1:])
    halves = jnp.broadcast_to(halves, (ALONG_X, *halves.shape[1:]))
    halves = halves.reshape(2 * ALONG_X, *halves.shape[2:])
    halves, gate, up = lax.optimization_barrier((halves, gate_matrix, up_matrix))
    gate_other, up_other = swap(gate, "core"), swap(up, "core")
    down_other = swap(down_matrix, "pair")
    got = lax.all_to_all(
        halves,
        ("far", "pair", "core"),
        0,
        0,
        tiled=True,
    )
    me, sources = core.reshape(1), PAIR * depth
    terms = up_product(0, me, got, sources, gate, up)
    terms = up_product(1, me, got, sources, gate_other, up_other, terms)
    arrived = lax.all_to_all(
        (terms * SCALE).astype(jnp.float16), ("pair", "z"), 0, 0, tiled=True
    )
    arrived = arrived.reshape(PAIR, depth, *arrived.shape[1:])
    total = jnp.sum(arrived.astype(jnp.float32), axis=1)
    hidden = activate(total, gate_matrix.shape[1])
    gathered = lax.all_gather(hidden, COL, axis=0, tiled=False)
    share = down_product(pair.reshape(1), gathered, down_matrix, down_other)
    return finish(lax.all_to_all(share, ("y", "far"), 0, 0, tiled=True))


def solution(mesh):
    n_row, n_col = mesh.devices.shape
    devices = mesh.devices.reshape(n_row // ALONG_X, FAR, PAIR, n_col // 2, 2)
    chips = jax.sharding.Mesh(devices, ROW + COL)
    placed = (P(ROW, COL), P(COL, ROW), P(COL, ROW), P(ROW, COL))
    return jax.shard_map(
        shards, mesh=chips, in_specs=placed, out_specs=P(ROW, COL), check_vma=False
    )
```

```python
import functools

import jax
import jax.numpy as jnp
from jax import lax
from jax.experimental import pallas as pl
from jax.experimental.pallas import tpu as pltpu
from jax.sharding import PartitionSpec as P

LANES = 128
MAIN = 16
EXTRA = 2
PAIR = 2
LIMIT = pltpu.CompilerParams(vmem_limit_bytes=8 * 1024 * 1024)
SCALAR = pl.BlockSpec(memory_space=pltpu.SMEM)
WHOLE = pl.BlockSpec(memory_space=pltpu.VMEM)
SCALE = 16.0
COST = 8
ROW, COL = ("y", "far", "pair"), ("z", "core")
ALONG_X = 4
FAR = ALONG_X // PAIR


def lanes(q):
    return slice(q * LANES, (q + 1) * LANES)


def rows_of(q, count):
    return slice(q * count, (q + 1) * count)


def gather_extra(tiles, shift_of):
    row = lax.broadcasted_iota(jnp.int32, tiles[0].shape, 0) // EXTRA
    out = tiles[0] if shift_of(0) % 8 == 0 else pltpu.roll(tiles[0], shift_of(0) % 8, 0)
    for q in range(1, len(tiles)):
        moved = tiles[q]
        if shift_of(q) % 8:
            moved = pltpu.roll(moved, shift_of(q) % 8, 0)
        out = jnp.where(row == q, moved, out)
    return out


def spread_kernel(x_ref, out_ref):
    x = x_ref[...].astype(jnp.float32)
    tiles = x.shape[1] // LANES
    for q in range(tiles):
        for r in range(out_ref.shape[0]):
            out_ref[r, rows_of(q, MAIN), :] = x_ref[:MAIN, lanes(q)]
    tail = jnp.concatenate(
        [x[MAIN:, lanes(q)] for q in range(tiles)], axis=0
    ).astype(jnp.bfloat16)
    for r in range(out_ref.shape[0]):
        out_ref[r, tiles * MAIN :, :] = tail


def spread(x, copies):
    rows = x.shape[0] * x.shape[1] // LANES
    return pl.pallas_call(
        spread_kernel,
        out_shape=jax.ShapeDtypeStruct((copies, rows, LANES), x.dtype),
        in_specs=[WHOLE],
        out_specs=WHOLE,
        compiler_params=LIMIT,
    )(x)


def add_product(source_at, ready, gate_ref, up_ref, base_ref, out_ref, held):
    sources = out_ref.shape[0]
    tiles = held.shape[1] // LANES
    wide_tiles = gate_ref.shape[1] // LANES
    main = sources * MAIN
    shape = (tiles * sources * 8, sources * 8)
    r = lax.broadcasted_iota(jnp.int32, shape, 0)
    c = lax.broadcasted_iota(jnp.int32, shape, 1)
    place = c == r // 8 % sources * 8 + r // (sources * 8) * EXTRA + r % EXTRA
    tails = []
    for n in range(sources):
        block = source_at(n)
        for q in range(tiles):
            held[rows_of(n, MAIN), lanes(q)] = block[rows_of(q, MAIN)]
        tails.append(block[tiles * MAIN :])
    moved = jnp.dot(
        place.astype(jnp.bfloat16),
        jnp.concatenate(tails, axis=0),
        preferred_element_type=jnp.float32,
    ).astype(jnp.bfloat16)
    for q in range(tiles):
        held[main:, lanes(q)] = moved[rows_of(q, sources * 8)]
    row = lax.broadcasted_iota(jnp.int32, (8, LANES), 0) // EXTRA
    x = held[...]
    for kind, weight_ref in enumerate((gate_ref, up_ref)):
        if kind:
            ready()
        for first in range(0, wide_tiles, 2):
            count = min(2, wide_tiles - first)
            columns = slice(first * LANES, (first + count) * LANES)
            term = jnp.dot(x, weight_ref[:, columns], preferred_element_type=jnp.float32)
            for n in range(sources):
                end = slice(main + n * 8, main + n * 8 + 8)
                start = 2 * wide_tiles * MAIN + 4 * first
                where = slice(start, start + 8)
                mixed = jnp.where(
                    row % 2 == 0, term[end, lanes(0)], term[end, lanes(count - 1)]
                )
                if base_ref is not None:
                    mixed += base_ref[n, where, :]
                if kind:
                    mixed = jnp.where(row < 2, out_ref[n, where, :], mixed)
                out_ref[n, where, :] = mixed
                for i in range(count):
                    where = rows_of(kind * wide_tiles + first + i, MAIN)
                    value = term[rows_of(n, MAIN), lanes(i)]
                    if base_ref is not None:
                        value += base_ref[n, where, :]
                    out_ref[n, where, :] = value


def up_kernel(flip, core_ref, got_ref, gate_ref, up_ref, *refs):
    base_ref, ready = None, lambda: None
    if flip:
        base_ref, out_ref, held, up_held, done = refs
        fetch = pltpu.make_async_copy(up_ref, up_held, done)
        fetch.start()
        up_ref, ready = up_held, fetch.wait
    else:
        out_ref, held = refs
    side = flip + (1 - 2 * flip) * core_ref[0]

    def source_at(n):
        b = n // PAIR
        return got_ref[(b % FAR * PAIR + n % PAIR) * 2 + side, b // FAR]

    add_product(source_at, ready, gate_ref, up_ref, base_ref, out_ref, held)


def up_product(flip, core, got, sources, gate, up, *base):
    wide_tiles = gate.shape[1] // LANES
    rows = 2 * wide_tiles * MAIN + (wide_tiles + 1) // 2 * 8
    work = COST * sources * (MAIN + 8) * gate.size
    held = [pltpu.VMEM((sources * (MAIN + 8), gate.shape[0]), jnp.bfloat16)]
    up_spec = WHOLE
    if flip:
        held += [pltpu.VMEM(up.shape, up.dtype), pltpu.SemaphoreType.DMA]
        up_spec = pl.BlockSpec(memory_space=pl.ANY)
    return pl.pallas_call(
        functools.partial(up_kernel, flip),
        cost_estimate=pl.CostEstimate(
            flops=4 * work, bytes_accessed=4 * gate.size, transcendentals=0
        ),
        out_shape=pltpu.VMEM((sources, rows, LANES), jnp.float32),
        in_specs=[SCALAR, WHOLE, WHOLE, up_spec] + [WHOLE] * len(base),
        out_specs=WHOLE,
        scratch_shapes=held,
        compiler_params=LIMIT,
    )(core, got, gate, up, *base)


def activate_kernel(sum_ref, out_ref):
    wide_tiles = out_ref.shape[0] // (PAIR * (MAIN + EXTRA))
    row = lax.broadcasted_iota(jnp.int32, (8, LANES), 0) // EXTRA

    def total(p, rows):
        return sum_ref[p, rows, :] * (1 / SCALE)

    for p in range(PAIR):
        for j in range(wide_tiles):
            gate = total(p, rows_of(j, MAIN))
            up = total(p, rows_of(wide_tiles + j, MAIN))
            out_ref[rows_of(j * PAIR + p, MAIN), :] = (
                gate / (1 + jnp.exp(-gate)) * up
            ).astype(jnp.bfloat16)
    for first in range(0, wide_tiles, 2):
        start = 2 * wide_tiles * MAIN + 4 * first
        tails = []
        for p in range(PAIR):
            mixed = total(p, slice(start, start + 8))
            tails.append(mixed / (1 + jnp.exp(-mixed)) * pltpu.roll(mixed, 4, 0))
        low, high = tails
        tail = jnp.where(row == 1, pltpu.roll(high, 2, 0), low)
        tail = jnp.where(row == 2, pltpu.roll(low, 2, 0), tail)
        tail = jnp.where(row == 3, pltpu.roll(high, 4, 0), tail)
        count = min(2, wide_tiles - first) * 4
        start = wide_tiles * PAIR * MAIN + 4 * first
        out_ref[start : start + count, :] = tail[:count].astype(jnp.bfloat16)


def activate(total, hidden_width):
    return pl.pallas_call(
        activate_kernel,
        out_shape=jax.ShapeDtypeStruct(
            (PAIR * (MAIN + EXTRA) * hidden_width // LANES, LANES), jnp.bfloat16
        ),
        in_specs=[WHOLE],
        out_specs=WHOLE,
        compiler_params=LIMIT,
    )(total)


def down_kernel(pair_ref, hidden_ref, own_ref, other_ref, out_ref, own, other):
    sources = hidden_ref.shape[0]
    main = sources * MAIN
    first = pair_ref[0] == 0
    wide_tiles = own.shape[1] // LANES
    for n in range(sources):
        for j in range(wide_tiles):
            a = hidden_ref[n, rows_of(j * PAIR, MAIN), :]
            b = hidden_ref[n, rows_of(j * PAIR + 1, MAIN), :]
            own[rows_of(n, MAIN), lanes(j)] = jnp.where(first, a, b)
            other[rows_of(n, MAIN), lanes(j)] = jnp.where(first, b, a)
        for j in range(0, wide_tiles, 2):
            count = min(2, wide_tiles - j)
            start = wide_tiles * PAIR * MAIN + 4 * j
            tail = hidden_ref[n, start : start + 4 * count, :]
            at = slice(main + n * 8, main + n * 8 + 4 * count)
            own[at, lanes(j)] = tail
            other[at, lanes(j)] = tail
            if count == 2:
                tail = pltpu.roll(tail.astype(jnp.float32), 4, 0).astype(jnp.bfloat16)
                own[at, lanes(j + 1)] = tail
                other[at, lanes(j + 1)] = tail
    tiles = own_ref.shape[1] // LANES
    mine = jnp.dot(own[...], own_ref[...], preferred_element_type=jnp.float32)
    theirs = jnp.dot(other[...], other_ref[...], preferred_element_type=jnp.float32)
    for n in range(sources):
        at, end = rows_of(n, MAIN), slice(main + n * 8, main + n * 8 + 8)
        to = n % 2 * (sources // 2) + n // 2
        tails = []
        for q in range(tiles):
            out_ref[to, rows_of(q, MAIN), :] = (
                mine[at, lanes(q)] + theirs[at, lanes(q)]
            ).astype(jnp.bfloat16)
            a, b = mine[end, lanes(q)], theirs[end, lanes(q)]
            later = pltpu.roll(jnp.where(first, b, a), 8 - EXTRA, 0)
            tails.append(jnp.where(first, a, b) + later)
        tail = gather_extra(tails, lambda q: q * EXTRA)
        out_ref[to, tiles * MAIN :, :] = tail.astype(jnp.bfloat16)


def down_product(pair, hidden, weight, other_weight):
    sources, width = hidden.shape[0], weight.shape[0]
    rows = (MAIN + EXTRA) * weight.shape[1] // LANES
    held = pltpu.VMEM((sources * (MAIN + 8), width), jnp.bfloat16)
    return pl.pallas_call(
        down_kernel,
        out_shape=jax.ShapeDtypeStruct((sources, rows, LANES), jnp.bfloat16),
        in_specs=[SCALAR] + [WHOLE] * 3,
        out_specs=WHOLE,
        scratch_shapes=[held, held],
        compiler_params=LIMIT,
    )(pair, hidden, weight, other_weight)


def finish_kernel(shares_ref, out_ref):
    tiles = out_ref.shape[1] // LANES
    total = shares_ref[0].astype(jnp.float32)
    for r in range(1, shares_ref.shape[0]):
        total += shares_ref[r].astype(jnp.float32)
    for q in range(tiles):
        out_ref[:MAIN, lanes(q)] = total[rows_of(q, MAIN)].astype(jnp.bfloat16)
        tail = total[tiles * MAIN + q * EXTRA : tiles * MAIN + (q + 1) * EXTRA]
        out_ref[MAIN:, lanes(q)] = tail.astype(jnp.bfloat16)


def finish(shares):
    width = shares.shape[1] // (MAIN + EXTRA) * LANES
    return pl.pallas_call(
        finish_kernel,
        out_shape=jax.ShapeDtypeStruct((MAIN + EXTRA, width), jnp.bfloat16),
        in_specs=[WHOLE],
        out_specs=WHOLE,
        compiler_params=LIMIT,
    )(shares)


def shards(activations, gate_matrix, up_matrix, down_matrix):
    n_row, depth = lax.axis_size(ROW), lax.axis_size("z")
    core, pair = lax.axis_index("core"), lax.axis_index("pair")

    def swap(x, axis):
        return lax.ppermute(x, axis, [(0, 1), (1, 0)])

    near = lax.all_to_all(
        spread(activations, n_row // ALONG_X), "y", 0, 0, tiled=True
    )
    halves = near.reshape(1, 2, near.shape[0] // 2, *near.shape[1:])
    halves = jnp.broadcast_to(halves, (ALONG_X, *halves.shape[1:]))
    halves = halves.reshape(2 * ALONG_X, *halves.shape[2:])
    halves, gate, up = lax.optimization_barrier((halves, gate_matrix, up_matrix))
    gate_other, up_other = swap(gate, "core"), swap(up, "core")
    down_other = swap(down_matrix, "pair")
    got = lax.all_to_all(
        halves,
        ("far", "pair", "core"),
        0,
        0,
        tiled=True,
    )
    me, sources = core.reshape(1), PAIR * depth
    terms = up_product(0, me, got, sources, gate, up)
    terms = up_product(1, me, got, sources, gate_other, up_other, terms)
    arrived = lax.all_to_all(
        (terms * SCALE).astype(jnp.float16), ("z", "pair"), 0, 0, tiled=True
    )
    arrived = arrived.reshape(depth, PAIR, *arrived.shape[1:])
    total = jnp.sum(arrived.astype(jnp.float32), axis=0)
    hidden = activate(total, gate_matrix.shape[1])
    gathered = lax.all_gather(hidden, COL, axis=0, tiled=False)
    share = down_product(pair.reshape(1), gathered, down_matrix, down_other)
    return finish(lax.all_to_all(share, ("y", "far"), 0, 0, tiled=True))


def solution(mesh):
    n_row, n_col = mesh.devices.shape
    devices = mesh.devices.reshape(n_row // ALONG_X, FAR, PAIR, n_col // 2, 2)
    chips = jax.sharding.Mesh(devices, ROW + COL)
    placed = (P(ROW, COL), P(COL, ROW), P(COL, ROW), P(ROW, COL))
    return jax.shard_map(
        shards, mesh=chips, in_specs=placed, out_specs=P(ROW, COL), check_vma=False
    )
```
